512 devices in a mesh: row: 16 (over z_lo, y), col: 32 (over x, z_hi, core).
Axes of the slice: x: 4, y: 4, z: 16 (z_hi: 4, z_lo: 4; z = z_hi * 4 + z_lo), core: 2. Of those that a mesh axis runs over, the one named last changes fastest.
Arguments:
- points: float32 [16, 65536], P(None, ('row', 'col')), may hold values from 0 to 1
- lengthscales: float32 [16], replicated, may hold values from 0.25 to 0.5
- variances: float32 [2], replicated, may hold values from 0.5 to 2
- factor: float32 [128, 65536], P(None, ('row', 'col')), may hold values from -0.5 to 0.5
- solution: float32 [16, 65536], P(None, ('row', 'col')), may hold values from -6 to 6
- residual: float32 [16, 65536], P(None, ('row', 'col')), may hold values from -48 to 48
- direction: float32 [16, 65536], P(None, ('row', 'col')), may hold values from -48 to 48
Outputs:
- new_solution: float32 [16, 65536], P(None, ('row', 'col'))
- new_residual: float32 [16, 65536], P(None, ('row', 'col'))
- new_direction: float32 [16, 65536], P(None, ('row', 'col'))
The draws below stay inside these ranges and needn't reach their ends.
All inputs are finite; a program needn't handle non-finite values.
Results may differ from the reference program's by a relative error of at most 0.0003.
Values sent between devices are 32-bit elements; how exact they have to be, the bound alone decides.
A program may use at most 64 MiB of HBM per device.

```python
import math
import jax
import jax.numpy as jnp
from jax import lax

INPUTS = 16
PROBES = 16
RANK = 128
POINTS = 65536


def draw_residual(key, part):
    key = jax.random.fold_in(key, 11)
    k_base = jax.random.fold_in(key, 0)
    k_point = jax.random.fold_in(key, 2)
    k_probe = jax.random.fold_in(key, 3)
    place = jnp.arange(POINTS, dtype=jnp.float32) / POINTS - 0.5
    point_scale = jnp.exp(jax.random.uniform(k_point, (1, POINTS), jnp.float32, -1.15, 1.15))
    probe_scale = jnp.exp(jax.random.uniform(k_probe, (PROBES, 1), jnp.float32, -1.15, 1.15))
    base = jnp.clip(jax.random.normal(k_base, (PROBES, POINTS), jnp.float32), -5.0, 5.0)
    trend = jnp.exp(1.1 * place)[None, :]
    return (0.5 * base * point_scale * probe_scale * trend).astype(jnp.float32)


def draw_direction(key, part):
    key = jax.random.fold_in(key, 12)
    k_base = jax.random.fold_in(key, 0)
    k_point = jax.random.fold_in(key, 2)
    k_probe = jax.random.fold_in(key, 3)
    place = jnp.arange(POINTS, dtype=jnp.float32) / POINTS - 0.5
    point_scale = jnp.exp(jax.random.uniform(k_point, (1, POINTS), jnp.float32, -1.15, 1.15))
    probe_scale = jnp.exp(jax.random.uniform(k_probe, (PROBES, 1), jnp.float32, -1.15, 1.15))
    base = jnp.clip(jax.random.normal(k_base, (PROBES, POINTS), jnp.float32), -5.0, 5.0)
    trend = jnp.exp(1.1 * place)[None, :]
    return (0.5 * base * point_scale * probe_scale * trend).astype(jnp.float32)


def draw_factor(key, part):
    key = jax.random.fold_in(key, 13)
    k_base = jax.random.fold_in(key, 0)
    k_point = jax.random.fold_in(key, 2)
    k_rank = jax.random.fold_in(key, 3)
    point_scale = jnp.exp(jax.random.uniform(k_point, (1, POINTS), jnp.float32, -1.15, 1.15))
    rank_scale = jnp.exp(jax.random.uniform(k_rank, (RANK, 1), jnp.float32, -1.15, 1.15))
    base = jnp.clip(jax.random.normal(k_base, (RANK, POINTS), jnp.float32), -5.0, 5.0)
    return (0.01 * base * point_scale * rank_scale).astype(jnp.float32)


def levels(own_key, dims, cuts, low, largest):
    def one(position, parts):
        draws = jax.random.uniform(jax.random.fold_in(jax.random.fold_in(own_key, 6), position), (parts,), jnp.float32, low / len(cuts), largest / len(cuts))
        return jnp.repeat(jnp.exp(draws), dims[position] // parts).reshape((-1,) + (1,) * (len(dims) - position - 1))

    level = one(*cuts[0])
    for cut in cuts[1:]:
        level = level * one(*cut)
    return level


def scatter_about(own_key, extent, deviation, limit, shards=(), kind=jnp.bfloat16):
    gain = levels(own_key, extent, shards, -0.22, 0.18) if shards else 1.0
    values = jax.random.normal(own_key, extent, jnp.float32) * deviation * gain
    return jnp.minimum(jnp.maximum(values, -limit), limit).astype(kind)


def setup_inputs(seed: int = 0) -> dict:
    key_of = jax.random.split(jax.random.key(seed), 8)
    return {
        "points": jnp.clip(1.0 * jax.random.uniform(key_of[0], (INPUTS, POINTS), jnp.float32) ** levels(key_of[0], (INPUTS, POINTS), ((1, 512),), -0.2, 0.2), 0.0, 1.0),
        "lengthscales": jnp.clip(jnp.exp(jax.random.uniform(key_of[1], (INPUTS,), jnp.float32, math.log(0.25), math.log(0.5))), 0.25, 0.5),
        "variances": jnp.clip(jax.random.uniform(key_of[2], (2,), jnp.float32, 0.5, 2.0), 0.5, 2.0),
        "factor": draw_factor(jax.random.fold_in(key_of[7], 71), 0),
        "solution": scatter_about(key_of[4], (PROBES, POINTS), 1.0, 6.0, ((1, 512),), jnp.float32),
        "residual": draw_residual(jax.random.fold_in(key_of[7], 71), 0),
        "direction": draw_direction(jax.random.fold_in(key_of[7], 71), 0),
    }


root_five = 5.0 ** 0.5
highest = lax.Precision.HIGHEST

def matern(cross, sq_left, sq_right, signal):
    dist_sq = jnp.maximum(sq_left[:, None] + sq_right[None, :] - 2.0 * cross, 0.0)
    dist = jnp.sqrt(dist_sq)
    return signal * (1.0 + root_five * dist + 5.0 / 3.0 * dist_sq) * jnp.exp(-root_five * dist)

def reference(points, lengthscales, variances, factor, solution, residual, direction):
    signal = variances[0]
    noise = variances[1]
    scaled = points / lengthscales[:, None]
    squares = lax.optimization_barrier(jnp.sum(scaled * scaled, axis=0))
    total = scaled.shape[1]
    probes = direction.shape[0]
    row_block = math.gcd(total, 2048)
    col_block = math.gcd(total, 8192)

    def one_rows(index):
        left = lax.dynamic_slice_in_dim(scaled, index * row_block, row_block, 1)
        left_sq = lax.dynamic_slice_in_dim(squares, index * row_block, row_block, 0)

        def col_step(acc, other):
            right = lax.dynamic_slice_in_dim(scaled, other * col_block, col_block, 1)
            right_sq = lax.dynamic_slice_in_dim(squares, other * col_block, col_block, 0)
            vectors = lax.dynamic_slice_in_dim(direction, other * col_block, col_block, 1)
            cross = lax.dot_general(left, right, (((0,), (0,)), ((), ())), precision=highest)
            kernel = matern(cross, left_sq, right_sq, signal)
            acc = acc + lax.dot_general(vectors, kernel, (((1,), (1,)), ((), ())), precision=highest)
            return (acc, None)
        start = jnp.zeros((probes, row_block), jnp.float32)
        acc, unused = lax.scan(col_step, start, jnp.arange(total // col_block, dtype=jnp.int32))
        return acc
    blocks = lax.map(one_rows, jnp.arange(total // row_block, dtype=jnp.int32))
    applied = jnp.transpose(blocks, (1, 0, 2)).reshape(probes, total)
    image = applied + noise * direction
    gram = jnp.dot(factor, factor.T, precision=highest)
    core = gram + noise * jnp.eye(factor.shape[0], dtype=jnp.float32)
    chol = jnp.linalg.cholesky(core)

    def precond(values):
        proj = jnp.dot(values, factor.T, precision=highest)
        coef = jax.scipy.linalg.cho_solve((chol, True), proj.T)
        return (values - jnp.dot(coef.T, factor, precision=highest)) / noise
    res_z = lax.optimization_barrier(jnp.sum(residual * precond(residual), axis=1))
    curvature = lax.optimization_barrier(jnp.sum(direction * image, axis=1))
    alpha = res_z / curvature
    new_solution = solution + alpha[:, None] * direction
    new_residual = residual - alpha[:, None] * image
    precond_new = precond(new_residual)
    res_z_new = lax.optimization_barrier(jnp.sum(new_residual * precond_new, axis=1))
    beta = res_z_new / res_z
    new_direction = precond_new + beta[:, None] * direction
    return (new_solution, new_residual, new_direction)
```

```python
import functools
import math

import jax
import jax.numpy as jnp
from jax import lax
from jax.experimental import pallas as pl
from jax.experimental.pallas import tpu as pltpu
from jax.sharding import PartitionSpec as P

F32 = jnp.float32
BF16 = jnp.bfloat16
MESH = pl.DeviceIdType.MESH
highest = lax.Precision.HIGHEST
NT = (((1,), (1,)), ((), ()))
X, Y, Z_HI, Z_LO = 4, 4, 4, 4
LN2 = math.log(2.0)
SCALE = math.sqrt(5.0) / LN2
POLY = LN2 * LN2 / 3.0
POLY_A = 3.0 / LN2
POLY_B = 3.0 / (LN2 * LN2)


def div(a, b):
    return a // b if isinstance(a, int) else lax.div(a, jnp.int32(b))


def rem(a, b):
    return a % b if isinstance(a, int) else lax.rem(a, jnp.int32(b))


def lanes(start, size):
    if isinstance(start, int):
        return slice(start, start + size)
    return pl.ds(pl.multiple_of(start, 128), size)


def split2(v):
    hi = v.astype(BF16)
    return hi, (v - hi.astype(F32)).astype(BF16)


def split3(v):
    hi = v.astype(BF16)
    left = v - hi.astype(F32)
    mid = left.astype(BF16)
    return hi, mid, (left - mid.astype(F32)).astype(BF16)


def matern(t_sq):
    t_sq = jnp.maximum(t_sq, 1e-30)
    t = t_sq * lax.rsqrt(t_sq)
    return (t * (t + POLY_A) + POLY_B) * jnp.exp2(-t)


def dot(a, b):
    return jnp.dot(a, b, preferred_element_type=F32)


def dot_nt(a, b):
    return lax.dot_general(a, b, NT, preferred_element_type=F32)


def shifts_of(nz):
    full = [d if d % 2 else -d for d in range(2, nz // 2)]
    pairs = [(full[i], full[i + 1]) for i in range(0, len(full), 2)]
    if len(pairs) > 1:
        pairs = [pairs[0]] + pairs[:0:-1]
    return pairs, nz // 2, 1


def kernel(
    points_ref, ls_ref, var_ref, factor_ref, solution_ref, residual_ref, direction_ref,
    sol_out, res_out, dir_out,
    item, items, zitems, a_mat, dp, bt, dq, btf, dqf,
    t_a, t_b, h_a, h_b, l_a, l_b, ft_a, ft_b, fh_a, fh_b, fl_a, fl_b,
    left, right, right_f, lsend, lrx, rsend, rrx,
    g_send, g_rx, g_piece, g_px, g_tot, g_all, core_ref,
    v_send, v_rx, v_piece, v_px, v_tot, v_all, projres_ref,
    send_sem, recv_sem,
):
    nz, npl = Z_HI * Z_LO, X * Y * 2
    tp = npl // 2
    pairs, half_shift, single = shifts_of(nz)
    probes = direction_ref.shape[0]
    row, col = lax.axis_index("row"), lax.axis_index("col")
    z = rem(div(col, 2), Z_HI) * Z_LO + div(row, Y)
    s = (div(col, 2 * Z_HI) * Y + rem(row, Y)) * 2 + rem(col, 2)

    def device(zz, ss):
        r = rem(zz, Z_LO) * Y + rem(div(ss, 2), Y)
        c = div(ss, 2 * Y) * (2 * Z_HI) + div(zz, Z_LO) * 2 + rem(ss, 2)
        return (r, c)

    def in_plane(j):
        return device(z, rem(s + j + npl, npl))

    def in_column(i):
        return device(rem(z + i + nz, nz), s)

    def send(kind, src, dst, target):
        pltpu.make_async_remote_copy(
            src_ref=src, dst_ref=dst, send_sem=send_sem.at[kind], recv_sem=recv_sem.at[kind],
            device_id=target, device_id_type=MESH,
        ).start()

    def wait(sem, kind, ref):
        pltpu.make_async_copy(ref, ref, sem.at[kind]).wait()

    def loop(lo, hi, body):
        def step(i, carry):
            body(i)
            return carry

        lax.fori_loop(lo, hi, step, 0)

    barrier = pltpu.get_barrier_semaphore()
    loop(1, npl, lambda j: pl.semaphore_signal(barrier, inc=1, device_id=in_plane(j), device_id_type=MESH))
    loop(1, nz, lambda i: pl.semaphore_signal(barrier, inc=1, device_id=in_column(i), device_id_type=MESH))

    sub16 = lax.broadcasted_iota(jnp.int32, (16, 128), 0)
    lane16 = lax.broadcasted_iota(jnp.int32, (16, 128), 1)
    scale = jnp.zeros((16, 128), F32)
    for i in range(16):
        scale = jnp.where(sub16 == i, ls_ref[i], scale)
    direction = direction_ref[...]
    residual = residual_ref[...]
    noise = var_ref[1]
    item[0:16, :] = (points_ref[...] - 0.5) / scale * SCALE
    item[16:32, :] = direction
    pl.semaphore_wait(barrier, npl + nz - 2)

    loop(1, npl, lambda j: send(0, item, items.at[j], in_plane(j)))
    shifts = [d for p in pairs for d in p] + [half_shift, single]
    slot_of = {d: i for i, d in enumerate(shifts)}
    z_order = sorted(shifts, key=lambda d: (d not in pairs[0] if pairs else False, abs(d)))
    for d in z_order:
        i = slot_of[d]
        pltpu.make_async_remote_copy(
            src_ref=item, dst_ref=zitems.at[i], send_sem=send_sem.at[1], recv_sem=recv_sem.at[10 + i],
            device_id=in_column(-d), device_id_type=MESH,
        ).start()

    factor = factor_ref[...]
    gram = lax.dot_general(factor, factor, NT, precision=highest, preferred_element_type=F32)
    g_send[...] = gram.reshape(g_send.shape)
    projres_ref[...] = lax.dot_general(residual, factor, NT, precision=highest, preferred_element_type=F32)
    loop(1, nz, lambda i: send(2, g_send.at[rem(z + i, nz)], g_rx.at[i], in_column(i)))

    def pieces(item_val):
        u, d = item_val[0:16], item_val[16:32]
        sq = jnp.sum(u * u, axis=0, keepdims=True)
        return split3(u), [v.astype(F32) for v in split3(sq)], split2(d)

    def tail(sq, first):
        out = jnp.zeros((16, 128), F32)
        for i in range(3):
            out = jnp.where(sub16 == first + i, sq[i], out)
        return jnp.where((sub16 >= 3 - first) & (sub16 < 6 - first), 1.0, out)

    def build_a(slot, item_val):
        (hi, mid, lo), sq, (dhi, dlo) = pieces(item_val)
        at = lanes(slot * 128, 128)
        for g, v in enumerate((hi, hi, mid, hi, lo, mid, tail(sq, 0).astype(BF16))):
            a_mat[g * 16 : g * 16 + 16, at] = v
        a_mat[112:128, at] = jnp.zeros((16, 128), BF16)
        dp[0:16, at] = dhi
        dp[16:32, at] = dlo

    def build_b(item_val):
        (hi, mid, lo), sq, (dhi, dlo) = pieces(item_val)
        hi, mid, lo = (-2.0 * v.astype(F32) for v in (hi, mid, lo))
        wide = jnp.concatenate([hi, mid, hi, lo, hi, mid, tail(sq, 3), jnp.zeros((16, 128), F32)], axis=0)
        return wide.T.astype(BF16), jnp.concatenate([dhi, dlo], axis=0)

    own = item[...]
    build_a(0, own)
    build_a(npl, own)
    b, d_b = build_b(own)
    bt[1, 0:128, :] = b
    dq[1, :, 0:128] = d_b
    right[...] = jnp.zeros_like(right)
    right_f[...] = jnp.zeros_like(right_f)
    left[1] = jnp.zeros(left.shape[1:], F32)

    def take_z(d, store):
        i = slot_of[d]
        wait(recv_sem, 10 + i, zitems.at[i])
        store(build_b(zitems[i]))

    def into(qt, half):
        def store(bd):
            bt[qt, half * 128 : half * 128 + 128, :] = bd[0]
            dq[qt, :, half * 128 : half * 128 + 128] = bd[1]

        return store

    def into_f(bd):
        btf[...] = bd[0]
        dqf[...] = bd[1]

    wait(recv_sem, 0, items.at[pl.ds(1, npl - 1)])
    loop(1, npl, lambda j: build_a(j, items[j]))

    def place(k):
        kk = k + (tp // 2) * div(k + 64 - 3 * tp // 2, 64)
        return div(kk, tp), rem(kk, tp)

    bufs = ((t_a, h_a, l_a), (t_b, h_b, l_b))

    def cross(k, par):
        qt, pt = place(k)
        bufs[par][0][...] = dot(bt[qt], a_mat[:, lanes(pt * 256, 256)])

    def elementwise(par):
        t, h, l = bufs[par]
        h[...], l[...] = split2(matern(t[...]))

    def apply(k, par):
        qt, pt = place(k)
        _, h, l = bufs[par]
        at = lanes(pt * 256, 256)
        d_q, d_p = dq[qt], dp[:, at]
        hi, lo = h[...], l[...]
        left[qt, :, at] = dot(d_q, hi) + dot(d_q, lo)
        right[qt] += dot_nt(d_p, hi) + dot_nt(d_p, lo)

    def steps(first, last):
        def one(k, par):
            apply(k - 2, par)
            elementwise(1 - par)
            cross(k, par)

        k = first
        if first == 0:
            cross(0, 0)
            elementwise(0)
            if last > 1:
                cross(1, 1)
            k = min(2, last)
        if (last - k) % 2 == 0 and last - k >= 4:

            def two(i):
                one(2 * i, 0)
                one(2 * i + 1, 1)

            loop(k // 2, last // 2, two)
        else:
            for kk in range(k, last):
                one(kk, kk % 2)

    def send_right(qt, halves):
        both = right[qt, 0:16, :] + right[qt, 16:32, :]
        for h, d in halves:
            i = slot_of[d]
            rsend[i] = both[:, h * 128 : h * 128 + 128]
            send(3, rsend.at[i], rrx.at[i], in_column(d))

    def gram_stage(stage):
        if stage == 0:
            wait(recv_sem, 2, g_rx.at[pl.ds(1, nz - 1)])
            total = g_send[z]
            for i in range(1, nz):
                total = total + g_rx[i]
            g_piece[...] = total
            loop(1, npl, lambda j: send(4, g_piece, g_px.at[j], in_plane(j)))
        elif stage == 1:
            wait(recv_sem, 4, g_px.at[pl.ds(1, npl - 1)])
            total = g_piece[...]
            for j in range(1, npl):
                total = total + g_px[j]
            g_tot[...] = total
            g_all[z] = total
            loop(1, nz, lambda i: send(5, g_tot, g_all.at[z], in_column(i)))
        else:
            wait(recv_sem, 5, g_rx.at[pl.ds(1, nz - 1)])
            eye = lax.broadcasted_iota(jnp.int32, (128, 128), 0) == lax.broadcasted_iota(jnp.int32, (128, 128), 1)
            core_ref[...] = g_all[...].reshape(128, 128) + jnp.where(eye, noise, 0.0)

    lane128 = lax.broadcasted_iota(jnp.int32, (128, 128), 1)
    sub128 = lax.broadcasted_iota(jnp.int32, (128, 128), 0)

    def sweep(k):
        m = core_ref[...]
        line = core_ref[pl.ds(k, 1), :]
        column = jnp.sum(jnp.where(lane128 == k, m, 0.0), axis=1, keepdims=True)
        pivot = jnp.sum(jnp.where(lane128[0:1] == k, line, 0.0), axis=1, keepdims=True)
        inv = 1.0 / pivot
        line = line * inv
        new = jnp.where(sub128 == k, line, m - column * line)
        core_ref[...] = jnp.where(lane128 == k, jnp.where(sub128 == k, -inv, column * inv), new)

    if pairs:
        take_z(pairs[0][0], into(0, 0))
        take_z(pairs[0][1], into(0, 1))
    steps(0, tp)
    gram_stage(0)
    take_z(half_shift, into(1, 1))
    steps(tp, tp + tp // 2)
    if pairs:
        send_right(0, ((0, pairs[0][0]), (1, pairs[0][1])))
    middle = lanes(tp * 128, 128)
    hi, lo = split2(matern(dot(bt[1], a_mat[:, middle])))
    d_p = dp[:, middle]
    right[1] += dot_nt(d_p, hi) + dot_nt(d_p, lo)
    gram_stage(1)
    end = tp + tp // 2
    for n, pair in enumerate(pairs[1:]):
        take_z(pair[0], into(2 + n, 0))
        take_z(pair[1], into(2 + n, 1))
        steps(end, end + tp)
        end += tp
        if n == 0:
            send_right(1, ((1, half_shift),))
        else:
            send_right(1 + n, ((0, pairs[n][0]), (1, pairs[n][1])))
    take_z(single, into_f)
    elementwise((end - 1) % 2)
    apply(end - 2, end % 2)
    apply(end - 1, (end - 1) % 2)
    if len(pairs) > 1:
        send_right(len(pairs), ((0, pairs[-1][0]), (1, pairs[-1][1])))
    else:
        send_right(1, ((1, half_shift),))
    gram_stage(2)

    fbufs = ((ft_a, fh_a, fl_a), (ft_b, fh_b, fl_b))

    def f_cross(k, par):
        fbufs[par][0][...] = dot(btf[...], a_mat[:, lanes(k * 512 + 128, 512)])

    def f_elementwise(par):
        t, h, l = fbufs[par]
        h[...], l[...] = split2(matern(t[...]))

    def f_apply(k, par, last=False):
        _, h, l = fbufs[par]
        d_q, d_p = dqf[...], dp[:, lanes(k * 512 + 128, 512)]
        hi, lo = h[...], l[...]
        out = dot(d_q, hi) + dot(d_q, lo)
        right_f[...] += dot_nt(d_p, hi) + dot_nt(d_p, lo)
        for i in range(4):
            j = k * 4 + 1 + i
            mine = last and i == 3
            total = out[0:16, i * 128 : i * 128 + 128] + out[16:32, i * 128 : i * 128 + 128]
            at = slice(0, 128) if mine else lanes(j * 128, 128)
            for qt in range(left.shape[0]):
                if not (mine and qt == 1) and not (qt == 0 and not pairs):
                    total = total + (left[qt, 0:16, at] + left[qt, 16:32, at])
            lsend[j] = total
            if not mine:
                send(6, lsend.at[j], lrx.at[npl - j], in_plane(-j))

    count = npl // 4

    def f_one(k, par):
        f_apply(k - 2, par)
        f_elementwise(1 - par)
        f_cross(k, par)

    f_cross(0, 0)
    f_elementwise(0)
    if count > 1:
        f_cross(1, 1)

        def f_two(i):
            f_one(2 * i, 0)
            f_one(2 * i + 1, 1)

        loop(1, count // 2, f_two)
        f_elementwise((count - 1) % 2)
        f_apply(count - 2, count % 2)
    f_apply(count - 1, (count - 1) % 2, last=True)
    i = slot_of[single]
    rsend[i] = right_f[0:16, :] + right_f[16:32, :]
    send(3, rsend.at[i], rrx.at[i], in_column(single))

    loop(0, 64, sweep)

    wait(recv_sem, 6, lrx.at[pl.ds(1, npl - 1)])
    wait(recv_sem, 3, rrx)
    total = lsend[npl] + (right[1, 0:16, 0:128] + right[1, 16:32, 0:128])
    for j in range(1, npl):
        total = total + lrx[j]
    for i in range(len(shifts)):
        total = total + rrx[i]
    image = (var_ref[0] * POLY) * total + noise * direction

    proj_im = lax.dot_general(image, factor, NT, precision=highest, preferred_element_type=F32)
    proj_re = projres_ref[...]
    scalars = jnp.zeros((16, 128), F32)
    for n, (a, b) in enumerate(((direction, image), (residual, image), (image, image), (residual, residual))):
        scalars = jnp.where(lane16 == n, jnp.sum(a * b, axis=1, keepdims=True), scalars)
    per = probes // nz
    for p in range(probes):
        for n, v in enumerate((proj_im, proj_re, scalars)):
            at = (p % per) * 4 + n
            v_send[p // per, at : at + 1, :] = v[p : p + 1, :]
        at = (p % per) * 4 + 3
        v_send[p // per, at : at + 1, :] = jnp.zeros((1, 128), F32)
    loop(1, nz, lambda i: send(7, v_send.at[rem(z + i, nz)], v_rx.at[i], in_column(i)))
    loop(64, 96, sweep)
    wait(recv_sem, 7, v_rx.at[pl.ds(1, nz - 1)])
    total = v_send[z]
    for i in range(1, nz):
        total = total + v_rx[i]
    v_piece[...] = total
    loop(1, npl, lambda j: send(8, v_piece, v_px.at[j], in_plane(j)))
    loop(96, 128, sweep)
    wait(recv_sem, 8, v_px.at[pl.ds(1, npl - 1)])
    total = v_piece[...]
    for j in range(1, npl):
        total = total + v_px[j]
    v_tot[...] = total
    v_all[z] = total
    loop(1, nz, lambda i: send(9, v_tot, v_all.at[z], in_column(i)))
    core_inv = -core_ref[...]
    wait(recv_sem, 9, v_rx.at[pl.ds(1, nz - 1)])

    def gathered(n):
        out = jnp.zeros((16, 128), F32)
        for p in range(probes):
            at = (p % per) * 4 + n
            out = jnp.where(sub16 == p, v_all[p // per, at : at + 1, :], out)
        return out

    proj_im, proj_re, scalars = gathered(0), gathered(1), gathered(2)
    d_im, r_im, im_im, r_r = (scalars[:, n : n + 1] for n in range(4))
    both = jnp.dot(
        jnp.concatenate([proj_re, proj_im], axis=0), core_inv, precision=highest, preferred_element_type=F32
    )
    coef_re, coef_im = both[0:16], both[16:32]
    res_z = (r_r - jnp.sum(proj_re * coef_re, axis=1, keepdims=True)) / noise
    alpha = res_z / d_im
    coef_new = coef_re - alpha * coef_im
    proj_new = proj_re - alpha * proj_im
    new_sq = r_r - 2.0 * alpha * r_im + alpha * alpha * im_im
    res_z_new = (new_sq - jnp.sum(proj_new * coef_new, axis=1, keepdims=True)) / noise
    beta = res_z_new / res_z
    new_residual = residual - alpha * image
    sol_out[...] = solution_ref[...] + alpha * direction
    res_out[...] = new_residual
    fitted = jnp.dot(coef_new, factor, precision=highest, preferred_element_type=F32)
    dir_out[...] = (new_residual - fitted) / noise + beta * direction

    wait(send_sem, 0, items.at[pl.ds(1, npl - 1)])
    wait(send_sem, 1, zitems)
    wait(send_sem, 2, g_rx.at[pl.ds(1, nz - 1)])
    wait(send_sem, 3, rrx)
    wait(send_sem, 4, g_px.at[pl.ds(1, npl - 1)])
    wait(send_sem, 5, g_rx.at[pl.ds(1, nz - 1)])
    wait(send_sem, 6, lrx.at[pl.ds(1, npl - 1)])
    wait(send_sem, 7, v_rx.at[pl.ds(1, nz - 1)])
    wait(send_sem, 8, v_px.at[pl.ds(1, npl - 1)])
    wait(send_sem, 9, v_rx.at[pl.ds(1, nz - 1)])


def local(points, lengthscales, variances, factor, solution, residual, direction):
    nz, npl = Z_HI * Z_LO, X * Y * 2
    pairs, _, _ = shifts_of(nz)
    blocks = 2 * len(pairs) + 2
    nq = 2 + max(len(pairs) - 1, 0)
    gr, vr = 128 // nz, 4 * (16 // nz)
    wide = (npl + 1) * 128
    vmem = pl.BlockSpec(memory_space=pltpu.VMEM)
    smem = pl.BlockSpec(memory_space=pltpu.SMEM)
    tile, ftile = (256, 256), (128, 512)
    scratch = [
        ((32, 128), F32), ((npl, 32, 128), F32), ((blocks, 32, 128), F32),
        ((128, wide), BF16), ((32, wide), BF16), ((nq, 256, 128), BF16), ((nq, 32, 256), BF16),
        ((128, 128), BF16), ((32, 128), BF16),
        (tile, F32), (tile, F32), (tile, BF16), (tile, BF16), (tile, BF16), (tile, BF16),
        (ftile, F32), (ftile, F32), (ftile, BF16), (ftile, BF16), (ftile, BF16), (ftile, BF16),
        ((nq, 32, npl * 128), F32), ((nq, 32, 256), F32), ((32, 128), F32),
        ((npl + 1, 16, 128), F32), ((npl, 16, 128), F32), ((blocks, 16, 128), F32), ((blocks, 16, 128), F32),
        ((nz, gr, 128), F32), ((nz, gr, 128), F32), ((gr, 128), F32), ((npl, gr, 128), F32),
        ((gr, 128), F32), ((nz, gr, 128), F32), ((128, 128), F32),
        ((nz, vr, 128), F32), ((nz, vr, 128), F32), ((vr, 128), F32), ((npl, vr, 128), F32),
        ((vr, 128), F32), ((nz, vr, 128), F32), ((16, 128), F32),
    ]
    out = jax.ShapeDtypeStruct(direction.shape, F32)
    return pl.pallas_call(
        kernel,
        out_shape=(out, out, out),
        in_specs=[vmem, smem, smem, vmem, vmem, vmem, vmem],
        out_specs=(vmem, vmem, vmem),
        scratch_shapes=[pltpu.VMEM(shape, dtype) for shape, dtype in scratch]
        + [pltpu.SemaphoreType.DMA((10,)), pltpu.SemaphoreType.DMA((10 + blocks,))],
        compiler_params=pltpu.CompilerParams(
            collective_id=0, has_side_effects=True, vmem_limit_bytes=40 * 2**20
        ),
    )(points, lengthscales, variances, factor, solution, residual, direction)


def solution(mesh):
    placed = P(None, ("row", "col"))
    return jax.shard_map(
        local,
        mesh=mesh,
        in_specs=(placed, P(), P(), placed, placed, placed, placed),
        out_specs=(placed, placed, placed),
        check_vma=False,
    )
```

```python
import functools
import math

import jax
import jax.numpy as jnp
from jax import lax
from jax.experimental import pallas as pl
from jax.experimental.pallas import tpu as pltpu
from jax.sharding import PartitionSpec as P

F32 = jnp.float32
BF16 = jnp.bfloat16
MESH = pl.DeviceIdType.MESH
highest = lax.Precision.HIGHEST
NT = (((1,), (1,)), ((), ()))
X, Y, Z_HI, Z_LO = 4, 4, 4, 4
LN2 = math.log(2.0)
SCALE = math.sqrt(5.0) / LN2
POLY = LN2 * LN2 / 3.0
POLY_A = 3.0 / LN2
POLY_B = 3.0 / (LN2 * LN2)


def div(a, b):
    return a // b if isinstance(a, int) else lax.div(a, jnp.int32(b))


def rem(a, b):
    return a % b if isinstance(a, int) else lax.rem(a, jnp.int32(b))


def lanes(start, size):
    if isinstance(start, int):
        return slice(start, start + size)
    return pl.ds(pl.multiple_of(start, 128), size)


def split2(v):
    hi = v.astype(BF16)
    return hi, (v - hi.astype(F32)).astype(BF16)


def split3(v):
    hi = v.astype(BF16)
    left = v - hi.astype(F32)
    mid = left.astype(BF16)
    return hi, mid, (left - mid.astype(F32)).astype(BF16)


def matern(t_sq):
    t_sq = jnp.maximum(t_sq, 1e-30)
    t = t_sq * lax.rsqrt(t_sq)
    return (t * (t + POLY_A) + POLY_B) * jnp.exp2(-t)


def dot(a, b):
    return jnp.dot(a, b, preferred_element_type=F32)


def dot_nt(a, b):
    return lax.dot_general(a, b, NT, preferred_element_type=F32)


def shifts_of(nz):
    full = [d if d % 2 else -d for d in range(2, nz // 2)]
    pairs = [(full[i], full[i + 1]) for i in range(0, len(full), 2)]
    if len(pairs) > 1:
        pairs = [pairs[0]] + pairs[:0:-1]
    return pairs, nz // 2, 1


def kernel(
    points_hbm, ls_hbm, var_hbm, factor_hbm, solution_hbm, residual_hbm, direction_hbm,
    sol_out, res_out, dir_out,
    points_ref, ls_ref, var_ref, factor_ref, solution_ref, residual_ref, direction_ref,
    item, items, zitems, a_mat, dp, bt, dq, btf, dqf,
    t_a, t_b, h_a, h_b, l_a, l_b, ft_a, ft_b, fh_a, fh_b, fl_a, fl_b,
    left, right, right_f, lsend, lrx, rsend, rrx,
    g_send, g_rx, g_piece, g_zx, g_tot, g_all, core_ref,
    v_give, v_take, v_chip, v_px, v_plane, v_zx, v_mine, v_all,
    in_sem, send_sem, recv_sem, item_sem,
):
    nz, npl = Z_HI * Z_LO, X * Y * 2
    tp = npl // 2
    pairs, half_shift, single = shifts_of(nz)
    probes = direction_hbm.shape[0]
    half_np = npl // 2
    row, col = lax.axis_index("row"), lax.axis_index("col")
    z = rem(div(col, 2), Z_HI) * Z_LO + div(row, Y)
    core = rem(col, 2)
    s = (div(col, 2 * Z_HI) * Y + rem(row, Y)) * 2 + core

    def device(zz, ss):
        r = rem(zz, Z_LO) * Y + rem(div(ss, 2), Y)
        c = div(ss, 2 * Y) * (2 * Z_HI) + div(zz, Z_LO) * 2 + rem(ss, 2)
        return (r, c)

    def in_plane(j):
        return device(z, rem(s + j + npl, npl))

    def other_core():
        return device(z, s + 1 - 2 * core)

    def in_column(i):
        return device(rem(z + i + nz, nz), s)

    def send(kind, src, dst, target):
        pltpu.make_async_remote_copy(
            src_ref=src, dst_ref=dst, send_sem=send_sem.at[kind], recv_sem=recv_sem.at[kind],
            device_id=target, device_id_type=MESH,
        ).start()

    def wait(sem, kind, ref):
        pltpu.make_async_copy(ref, ref, sem.at[kind]).wait()

    def loop(lo, hi, body):
        def step(i, carry):
            body(i)
            return carry

        lax.fori_loop(lo, hi, step, 0)

    barrier = pltpu.get_barrier_semaphore()
    loop(1, npl, lambda j: pl.semaphore_signal(barrier, inc=1, device_id=in_plane(j), device_id_type=MESH))
    loop(1, nz, lambda i: pl.semaphore_signal(barrier, inc=1, device_id=in_column(i), device_id_type=MESH))

    loads = [
        pltpu.make_async_copy(src, dst, in_sem.at[i])
        for i, (src, dst) in enumerate((
            (ls_hbm, ls_ref), (var_hbm, var_ref), (points_hbm, points_ref), (direction_hbm, direction_ref),
            (factor_hbm, factor_ref), (residual_hbm, residual_ref), (solution_hbm, solution_ref),
        ))
    ]
    for load in loads:
        load.start()
    for load in loads:
        load.wait()

    sub16 = lax.broadcasted_iota(jnp.int32, (16, 128), 0)
    lane16 = lax.broadcasted_iota(jnp.int32, (16, 128), 1)
    scale = jnp.zeros((16, 128), F32)
    for i in range(16):
        scale = jnp.where(sub16 == i, ls_ref[i], scale)
    direction = direction_ref[...]
    residual = residual_ref[...]
    noise = var_ref[1]
    item[0:16, :] = (points_ref[...] - 0.5) / scale * SCALE
    item[16:32, :] = direction
    pl.semaphore_wait(barrier, npl + nz - 2)

    def give(src, position, target):
        pltpu.make_async_remote_copy(
            src_ref=src, dst_ref=items.at[position], send_sem=send_sem.at[0], recv_sem=item_sem.at[position],
            device_id=target, device_id_type=MESH,
        ).start()

    def at_other_core(position):
        return half_np + rem(position + (half_np - 1) * core, half_np)

    shifts = [d for p in pairs for d in p] + [half_shift, single]
    slot_of = {d: i for i, d in enumerate(shifts)}
    z_order = sorted(shifts, key=lambda d: (d not in pairs[0] if pairs else False, -abs(d)))
    for d in z_order:
        i = slot_of[d]
        pltpu.make_async_remote_copy(
            src_ref=item, dst_ref=zitems.at[i], send_sem=send_sem.at[1], recv_sem=recv_sem.at[11 + i],
            device_id=in_column(-d), device_id_type=MESH,
        ).start()
    give(item, at_other_core(0), other_core())
    loop(1, half_np, lambda m: give(item, m, in_plane(2 * m)))

    factor = factor_ref[...]
    gram = lax.dot_general(factor, factor, NT, precision=highest, preferred_element_type=F32)
    g_rows, per = 128 // npl, max(probes // npl, 1)
    proj = lax.dot_general(residual, factor, NT, precision=highest, preferred_element_type=F32)
    g_pad = g_send.shape[1] - g_rows - per
    for i in range(npl):
        g_send[i, 0:g_rows, :] = gram[i * g_rows : i * g_rows + g_rows]
        if i * per < probes:
            g_send[i, g_rows : g_rows + per, :] = proj[i * per : i * per + per]
        else:
            g_send[i, g_rows : g_rows + per, :] = jnp.zeros((per, 128), F32)
        g_send[i, g_rows + per :, :] = jnp.zeros((g_pad, 128), F32)
    loop(1, npl, lambda j: send(2, g_send.at[rem(s + j, npl)], g_rx.at[j], in_plane(j)))

    def pieces(item_val):
        u, d = item_val[0:16], item_val[16:32]
        sq = jnp.sum(u * u, axis=0, keepdims=True)
        return split3(u), [v.astype(F32) for v in split3(sq)], split2(d)

    def tail(sq, first):
        out = jnp.zeros((16, 128), F32)
        for i in range(3):
            out = jnp.where(sub16 == first + i, sq[i], out)
        return jnp.where((sub16 >= 3 - first) & (sub16 < 6 - first), 1.0, out)

    def build_a(slot, item_val):
        (hi, mid, lo), sq, (dhi, dlo) = pieces(item_val)
        at = lanes(slot * 128, 128)
        for g, v in enumerate((hi, hi, mid, hi, lo, mid, tail(sq, 0).astype(BF16))):
            a_mat[g * 16 : g * 16 + 16, at] = v
        a_mat[112:128, at] = jnp.zeros((16, 128), BF16)
        dp[0:16, at] = dhi
        dp[16:32, at] = dlo

    def build_b(item_val):
        (hi, mid, lo), sq, (dhi, dlo) = pieces(item_val)
        hi, mid, lo = (-2.0 * v.astype(F32) for v in (hi, mid, lo))
        wide = jnp.concatenate([hi, mid, hi, lo, hi, mid, tail(sq, 3), jnp.zeros((16, 128), F32)], axis=0)
        return wide.T.astype(BF16), jnp.concatenate([dhi, dlo], axis=0)

    own = item[...]
    build_a(0, own)
    build_a(npl, own)
    b, d_b = build_b(own)
    bt[1, 0:128, :] = b
    dq[1, :, 0:128] = d_b
    right[...] = jnp.zeros_like(right)
    right_f[...] = jnp.zeros_like(right_f)
    left[1] = jnp.zeros(left.shape[1:], F32)

    def take_z(d, store):
        i = slot_of[d]
        wait(recv_sem, 11 + i, zitems.at[i])
        store(build_b(zitems[i]))

    def into(qt, half):
        def store(bd):
            bt[qt, half * 128 : half * 128 + 128, :] = bd[0]
            dq[qt, :, half * 128 : half * 128 + 128] = bd[1]

        return store

    def into_f(bd):
        btf[...] = bd[0]
        dqf[...] = bd[1]

    def prepare(k):
        for i in range(2):
            position = 2 * k + i
            if isinstance(position, int) and position == 0:
                continue
            here = items.at[position]
            pltpu.make_async_copy(here, here, item_sem.at[position]).wait()
            yield position

    def prepare_even(k):
        for position in prepare(k):
            give(items.at[position], at_other_core(position), other_core())
            build_a(position, items[position])

    def prepare_odd(k):
        for position in prepare(k):
            build_a(position, items[position])

    def place(k):
        kk = k + (tp // 2) * div(k + 64 - 3 * tp // 2, 64)
        qt, r = div(kk, tp), rem(kk, tp)
        is_half = div(qt + 2, 3) * div(4 - qt, 3)
        return qt, r + is_half * (tp // 4) * div(r, tp // 4)

    bufs = ((t_a, h_a, l_a), (t_b, h_b, l_b))

    def cross(k, par):
        qt, pt = place(k)
        bufs[par][0][...] = dot(bt[qt], a_mat[:, lanes(pt * 256, 256)])

    def elementwise(par):
        t, h, l = bufs[par]
        h[...], l[...] = split2(matern(t[...]))

    def apply(k, par):
        qt, pt = place(k)
        _, h, l = bufs[par]
        at = lanes(pt * 256, 256)
        d_q, d_p = dq[qt], dp[:, at]
        hi, lo = h[...], l[...]
        left[qt, :, at] = dot(d_q, hi) + dot(d_q, lo)
        right[qt] += dot_nt(d_p, hi) + dot_nt(d_p, lo)

    def steps(first, last, prepared=None):
        def one(k, par):
            if prepared:
                prepared(k)
            apply(k - 2, par)
            elementwise(1 - par)
            cross(k, par)

        k = first
        if first == 0:
            prepared(0)
            cross(0, 0)
            prepared(1)
            elementwise(0)
            cross(1, 1)
            k = 2
        if (last - k) % 2 == 0 and last - k >= 4:

            def two(i):
                one(2 * i, 0)
                one(2 * i + 1, 1)

            loop(k // 2, last // 2, two)
        else:
            for kk in range(k, last):
                one(kk, kk % 2)

    def send_right(qt, halves):
        both = right[qt, 0:16, :] + right[qt, 16:32, :]
        for h, d in halves:
            i = slot_of[d]
            rsend[i] = both[:, h * 128 : h * 128 + 128]
            send(3, rsend.at[i], rrx.at[i], in_column(d))

    def gram_stage(stage):
        if stage == 0:
            wait(recv_sem, 2, g_rx.at[pl.ds(1, npl - 1)])
            total = g_send[s]
            for j in range(1, npl):
                total = total + g_rx[j]
            g_piece[...] = total
            loop(1, nz, lambda i: send(4, g_piece, g_zx.at[i], in_column(i)))
        elif stage == 1:
            wait(recv_sem, 4, g_zx.at[pl.ds(1, nz - 1)])
            total = g_piece[...]
            for i in range(1, nz):
                total = total + g_zx[i]
            g_tot[...] = total
            g_all[s] = total
            loop(1, npl, lambda j: send(5, g_tot, g_all.at[s], in_plane(j)))
        else:
            wait(recv_sem, 5, g_rx.at[pl.ds(1, npl - 1)])
            eye = lax.broadcasted_iota(jnp.int32, (128, 128), 0) == lax.broadcasted_iota(jnp.int32, (128, 128), 1)
            gram = jnp.concatenate([g_all[i, 0:g_rows, :] for i in range(npl)], axis=0)
            core_ref[...] = gram + jnp.where(eye, noise, 0.0)

    lane128 = lax.broadcasted_iota(jnp.int32, (128, 128), 1)
    sub128 = lax.broadcasted_iota(jnp.int32, (128, 128), 0)

    def sweep(k):
        m = core_ref[...]
        line = core_ref[pl.ds(k, 1), :]
        column = jnp.sum(jnp.where(lane128 == k, m, 0.0), axis=1, keepdims=True)
        pivot = jnp.sum(jnp.where(lane128[0:1] == k, line, 0.0), axis=1, keepdims=True)
        inv = 1.0 / pivot
        line = line * inv
        new = jnp.where(sub128 == k, line, m - column * line)
        core_ref[...] = jnp.where(lane128 == k, jnp.where(sub128 == k, -inv, column * inv), new)

    if pairs:
        take_z(pairs[0][0], into(0, 0))
        take_z(pairs[0][1], into(0, 1))
    steps(0, tp // 2, prepare_even)
    steps(tp // 2, tp, prepare_odd)
    gram_stage(0)
    take_z(half_shift, into(1, 1))
    steps(tp, tp + tp // 2)
    if pairs:
        send_right(0, ((0, pairs[0][0]), (1, pairs[0][1])))
    middle = lanes(npl // 4 * 128, 128)
    hi, lo = split2(matern(dot(bt[1], a_mat[:, middle])))
    d_p = dp[:, middle]
    right[1] += dot_nt(d_p, hi) + dot_nt(d_p, lo)
    end = tp + tp // 2
    for n, pair in enumerate(pairs[1:]):
        take_z(pair[0], into(2 + n, 0))
        take_z(pair[1], into(2 + n, 1))
        steps(end, end + tp)
        end += tp
        if n == 0:
            send_right(1, ((1, half_shift),))
        else:
            send_right(1 + n, ((0, pairs[n][0]), (1, pairs[n][1])))
    take_z(single, into_f)
    elementwise((end - 1) % 2)
    apply(end - 2, end % 2)
    apply(end - 1, (end - 1) % 2)
    if len(pairs) > 1:
        send_right(len(pairs), ((0, pairs[-1][0]), (1, pairs[-1][1])))
    else:
        send_right(1, ((1, half_shift),))
    gram_stage(1)

    fbufs = ((ft_a, fh_a, fl_a), (ft_b, fh_b, fl_b))

    def f_cross(k, par):
        fbufs[par][0][...] = dot(btf[...], a_mat[:, lanes(k * 512 + 128, 512)])

    def f_elementwise(par):
        t, h, l = fbufs[par]
        h[...], l[...] = split2(matern(t[...]))

    def f_apply(k, par, last=False):
        _, h, l = fbufs[par]
        d_q, d_p = dqf[...], dp[:, lanes(k * 512 + 128, 512)]
        hi, lo = h[...], l[...]
        out = dot(d_q, hi) + dot(d_q, lo)
        right_f[...] += dot_nt(d_p, hi) + dot_nt(d_p, lo)
        for i in range(4):
            j = k * 4 + 1 + i
            mine = last and i == 3
            total = out[0:16, i * 128 : i * 128 + 128] + out[16:32, i * 128 : i * 128 + 128]
            at = slice(0, 128) if mine else lanes(j * 128, 128)
            for qt in range(left.shape[0]):
                if not (mine and qt == 1) and not (qt == 0 and not pairs):
                    total = total + (left[qt, 0:16, at] + left[qt, 16:32, at])
            lsend[j] = total
            if not mine:
                slot = 2 * rem(j, half_np) + div(j, half_np)
                send(6, lsend.at[j], lrx.at[npl - slot], in_plane(-slot))

    count = npl // 4

    def f_one(k, par):
        f_apply(k - 2, par)
        f_elementwise(1 - par)
        f_cross(k, par)

    f_cross(0, 0)
    f_elementwise(0)
    if count > 1:
        f_cross(1, 1)

        def f_two(i):
            f_one(2 * i, 0)
            f_one(2 * i + 1, 1)

        loop(1, count // 2, f_two)
        f_elementwise((count - 1) % 2)
        f_apply(count - 2, count % 2)
    f_apply(count - 1, (count - 1) % 2, last=True)
    i = slot_of[single]
    rsend[i] = right_f[0:16, :] + right_f[16:32, :]
    send(3, rsend.at[i], rrx.at[i], in_column(single))

    wait(recv_sem, 6, lrx.at[pl.ds(1, npl - 1)])
    wait(recv_sem, 3, rrx)
    total = lsend[npl] + (right[1, 0:16, 0:128] + right[1, 16:32, 0:128])
    for j in range(1, npl):
        total = total + lrx[j]
    for i in range(len(shifts)):
        total = total + rrx[i]
    image = (var_ref[0] * POLY) * total + noise * direction

    proj_im = lax.dot_general(image, factor, NT, precision=highest, preferred_element_type=F32)
    products = ((direction, image), (residual, image), (image, image), (residual, residual))
    scalars = jnp.zeros((16, 128), F32)
    for n, (a, b) in enumerate(products):
        scalars = jnp.where(lane16 == rem(sub16, 8) * 4 + n, jnp.sum(a * b, axis=1, keepdims=True), scalars)

    def half_of(c):
        first = c == 0
        rows = jnp.where(first, proj_im[0:8], proj_im[8:16])
        inner = jnp.where(first, scalars[0:8], scalars[8:16])
        return rows, jnp.sum(inner, axis=0, keepdims=True)

    for ref, (rows, inner) in ((v_give, half_of(1 - core)), (v_chip, half_of(core))):
        for p in range(8):
            ref[p] = rows[p : p + 1]
        ref[8] = inner
    send(7, v_give, v_take, other_core())
    wait(recv_sem, 7, v_take)
    v_chip[...] += v_take[...]
    loop(1, half_np, lambda m: send(8, v_chip, v_px.at[m], in_plane(2 * m)))
    gram_stage(2)
    loop(0, 44, sweep)
    wait(recv_sem, 8, v_px.at[pl.ds(1, half_np - 1)])
    total = v_chip[...]
    for m in range(1, half_np):
        total = total + v_px[m]
    v_plane[...] = total
    loop(1, nz, lambda i: send(9, v_plane, v_zx.at[i], in_column(i)))
    loop(44, 128, sweep)
    wait(recv_sem, 9, v_zx.at[pl.ds(1, nz - 1)])
    total = v_plane[...]
    for i in range(1, nz):
        total = total + v_zx[i]
    v_mine[...] = total
    v_all[core] = total
    send(10, v_mine, v_all.at[core], other_core())
    core_inv = -core_ref[...]
    proj_re = jnp.zeros((16, 128), F32)
    for p in range(probes):
        at = g_rows + p % per
        proj_re = jnp.where(sub16 == p, g_all[p // per, at : at + 1, :], proj_re)
    wait(recv_sem, 10, v_take)
    proj_im = jnp.zeros((16, 128), F32)
    for p in range(probes):
        proj_im = jnp.where(sub16 == p, v_all[p // 8, p % 8], proj_im)
    inner = jnp.where(sub16 < 8, v_all[0, 8], v_all[1, 8])
    d_im, r_im, im_im, r_r = (
        jnp.sum(jnp.where(lane16 == rem(sub16, 8) * 4 + n, inner, 0.0), axis=1, keepdims=True) for n in range(4)
    )
    both = jnp.dot(
        jnp.concatenate([proj_re, proj_im], axis=0), core_inv, precision=highest, preferred_element_type=F32
    )
    coef_re, coef_im = both[0:16], both[16:32]
    res_z = (r_r - jnp.sum(proj_re * coef_re, axis=1, keepdims=True)) / noise
    alpha = res_z / d_im
    coef_new = coef_re - alpha * coef_im
    proj_new = proj_re - alpha * proj_im
    new_sq = r_r - 2.0 * alpha * r_im + alpha * alpha * im_im
    res_z_new = (new_sq - jnp.sum(proj_new * coef_new, axis=1, keepdims=True)) / noise
    beta = res_z_new / res_z
    new_residual = residual - alpha * image
    sol_out[...] = solution_ref[...] + alpha * direction
    res_out[...] = new_residual
    fitted = jnp.dot(coef_new, factor, precision=highest, preferred_element_type=F32)
    dir_out[...] = (new_residual - fitted) / noise + beta * direction

    wait(send_sem, 0, items.at[pl.ds(1, npl - 1)])
    wait(send_sem, 1, zitems)
    wait(send_sem, 2, g_rx.at[pl.ds(1, npl - 1)])
    wait(send_sem, 3, rrx)
    wait(send_sem, 4, g_zx.at[pl.ds(1, nz - 1)])
    wait(send_sem, 5, g_rx.at[pl.ds(1, npl - 1)])
    wait(send_sem, 6, lrx.at[pl.ds(1, npl - 1)])
    wait(send_sem, 7, v_take)
    wait(send_sem, 8, v_px.at[pl.ds(1, half_np - 1)])
    wait(send_sem, 9, v_zx.at[pl.ds(1, nz - 1)])
    wait(send_sem, 10, v_take)


def hand_out(*refs):
    for src, dst in zip(refs[:3], refs[3:]):
        dst[...] = src[...]


def local(points, lengthscales, variances, factor, solution, residual, direction):
    nz, npl = Z_HI * Z_LO, X * Y * 2
    pairs, _, _ = shifts_of(nz)
    blocks = 2 * len(pairs) + 2
    nq = 2 + max(len(pairs) - 1, 0)
    gr, vr = -(-(128 // npl + max(16 // npl, 1)) // 8) * 8, (9, 1, 128)
    wide = (npl + 1) * 128
    vmem = pl.BlockSpec(memory_space=pltpu.VMEM)
    held = [pltpu.VMEM, pltpu.SMEM, pltpu.SMEM, pltpu.VMEM, pltpu.VMEM, pltpu.VMEM, pltpu.VMEM]
    args = (points, lengthscales, variances, factor, solution, residual, direction)
    tile, ftile = (256, 256), (128, 512)
    scratch = [
        ((32, 128), F32), ((npl, 32, 128), F32), ((blocks, 32, 128), F32),
        ((128, wide), BF16), ((32, wide), BF16), ((nq, 256, 128), BF16), ((nq, 32, 256), BF16),
        ((128, 128), BF16), ((32, 128), BF16),
        (tile, F32), (tile, F32), (tile, BF16), (tile, BF16), (tile, BF16), (tile, BF16),
        (ftile, F32), (ftile, F32), (ftile, BF16), (ftile, BF16), (ftile, BF16), (ftile, BF16),
        ((nq, 32, npl * 128), F32), ((nq, 32, 256), F32), ((32, 128), F32),
        ((npl + 1, 16, 128), F32), ((npl, 16, 128), F32), ((blocks, 16, 128), F32), ((blocks, 16, 128), F32),
        ((npl, gr, 128), F32), ((npl, gr, 128), F32), ((gr, 128), F32), ((nz, gr, 128), F32),
        ((gr, 128), F32), ((npl, gr, 128), F32), ((128, 128), F32),
        (vr, F32), (vr, F32), (vr, F32), ((npl // 2, *vr), F32), (vr, F32), ((nz, *vr), F32), (vr, F32), ((2, *vr), F32),
    ]
    out = jax.ShapeDtypeStruct(direction.shape, F32)
    outs = pl.pallas_call(
        kernel,
        out_shape=(out, out, out),
        in_specs=[pl.BlockSpec(memory_space=pl.ANY)] * len(args),
        out_specs=(vmem, vmem, vmem),
        scratch_shapes=[space(a.shape, F32) for space, a in zip(held, args)]
        + [pltpu.VMEM(shape, dtype) for shape, dtype in scratch]
        + [pltpu.SemaphoreType.DMA((n,)) for n in (len(args), 11, 11 + blocks, npl)],
        compiler_params=pltpu.CompilerParams(
            collective_id=0, has_side_effects=True, vmem_limit_bytes=56 * 2**20
        ),
    )(*args)
    return pl.pallas_call(
        hand_out,
        out_shape=(out, out, out),
        in_specs=[vmem] * 3,
        out_specs=(vmem, vmem, vmem),
    )(*outs)


def solution(mesh):
    placed = P(None, ("row", "col"))
    return jax.shard_map(
        local,
        mesh=mesh,
        in_specs=(placed, P(), P(), placed, placed, placed, placed),
        out_specs=(placed, placed, placed),
        check_vma=False,
    )
```

```python
import functools
import math

import jax
import jax.numpy as jnp
from jax import lax
from jax.experimental import pallas as pl
from jax.experimental.pallas import tpu as pltpu
from jax.sharding import PartitionSpec as P

F32 = jnp.float32
BF16 = jnp.bfloat16
MESH = pl.DeviceIdType.MESH
highest = lax.Precision.HIGHEST
NT = (((1,), (1,)), ((), ()))
X, Y, Z_HI, Z_LO = 4, 4, 4, 4
LN2 = math.log(2.0)
SCALE = math.sqrt(5.0) / LN2
POLY = LN2 * LN2 / 3.0
POLY_A = 3.0 / LN2
POLY_B = 3.0 / (LN2 * LN2)


def div(a, b):
    return a // b if isinstance(a, int) else lax.div(a, jnp.int32(b))


def rem(a, b):
    return a % b if isinstance(a, int) else lax.rem(a, jnp.int32(b))


def lanes(start, size):
    if isinstance(start, int):
        return slice(start, start + size)
    return pl.ds(pl.multiple_of(start, 128), size)


def split2(v):
    hi = v.astype(BF16)
    return hi, (v - hi.astype(F32)).astype(BF16)


def split3(v):
    hi = v.astype(BF16)
    left = v - hi.astype(F32)
    mid = left.astype(BF16)
    return hi, mid, (left - mid.astype(F32)).astype(BF16)


def matern(t_sq):
    t_sq = jnp.maximum(t_sq, 1e-30)
    t = t_sq * lax.rsqrt(t_sq)
    return (t * (t + POLY_A) + POLY_B) * jnp.exp2(-t)


def dot(a, b):
    return jnp.dot(a, b, preferred_element_type=F32)


def dot_nt(a, b):
    return lax.dot_general(a, b, NT, preferred_element_type=F32)


PLANES = {16: (((2, 3), (-6, -7), (-5, 4)), -8, 1), 8: (((2, -3),), -4, 1)}


def kernel(
    points_hbm, ls_hbm, var_hbm, factor_hbm, solution_hbm, residual_hbm, direction_hbm,
    sol_out, res_out, dir_out,
    points_ref, ls_ref, var_ref, factor_ref, solution_ref, residual_ref, direction_ref,
    item, items, zitems, hub_item, a_mat, dp, bt, dq, btf, dqf,
    t_a, t_b, h_a, h_b, l_a, l_b, ft_a, ft_b, fh_a, fh_b, fl_a, fl_b,
    left, right, right_f, lsend, lrx, rsend, rrx, hub_rx, hub_out, hub_in,
    g_send, g_rx, g_piece, g_zx, g_window, g_zy, g_tot, g_all, core_ref,
    v_give, v_take, v_chip, v_px, v_plane, v_zx, v_window, v_zy, v_mine, v_all,
    in_sem, send_sem, recv_sem, item_sem,
):
    nz, npl = Z_HI * Z_LO, X * Y * 2
    tp = npl // 2
    pairs, half_shift, single = PLANES[nz]
    quarter = nz // 4
    probes = direction_hbm.shape[0]
    half_np = npl // 2
    row, col = lax.axis_index("row"), lax.axis_index("col")
    z = rem(div(col, 2), Z_HI) * Z_LO + div(row, Y)
    core = rem(col, 2)
    s = (div(col, 2 * Z_HI) * Y + rem(row, Y)) * 2 + core

    def device(zz, ss):
        r = rem(zz, Z_LO) * Y + rem(div(ss, 2), Y)
        c = div(ss, 2 * Y) * (2 * Z_HI) + div(zz, Z_LO) * 2 + rem(ss, 2)
        return (r, c)

    def in_plane(j):
        return device(z, rem(s + j + npl, npl))

    def other_core():
        return device(z, s + 1 - 2 * core)

    def in_column(i):
        return device(rem(z + i + nz, nz), s)

    def send(kind, src, dst, target):
        pltpu.make_async_remote_copy(
            src_ref=src, dst_ref=dst, send_sem=send_sem.at[kind], recv_sem=recv_sem.at[kind],
            device_id=target, device_id_type=MESH,
        ).start()

    def wait(sem, kind, ref):
        pltpu.make_async_copy(ref, ref, sem.at[kind]).wait()

    def loop(lo, hi, body):
        def step(i, carry):
            body(i)
            return carry

        lax.fori_loop(lo, hi, step, 0)

    barrier = pltpu.get_barrier_semaphore()
    loop(1, npl, lambda j: pl.semaphore_signal(barrier, inc=1, device_id=in_plane(j), device_id_type=MESH))
    for sign in (1, -1):
        loop(
            1,
            quarter + 1,
            lambda i, sign=sign: pl.semaphore_signal(
                barrier, inc=1, device_id=in_column(sign * i), device_id_type=MESH
            ),
        )

    loads = [
        pltpu.make_async_copy(src, dst, in_sem.at[i])
        for i, (src, dst) in enumerate((
            (ls_hbm, ls_ref), (var_hbm, var_ref), (points_hbm, points_ref), (direction_hbm, direction_ref),
            (factor_hbm, factor_ref), (residual_hbm, residual_ref), (solution_hbm, solution_ref),
        ))
    ]
    for load in loads:
        load.start()
    for load in loads:
        load.wait()

    sub16 = lax.broadcasted_iota(jnp.int32, (16, 128), 0)
    lane16 = lax.broadcasted_iota(jnp.int32, (16, 128), 1)
    scale = jnp.zeros((16, 128), F32)
    for i in range(16):
        scale = jnp.where(sub16 == i, ls_ref[i], scale)
    direction = direction_ref[...]
    residual = residual_ref[...]
    noise = var_ref[1]
    item[0:16, :] = (points_ref[...] - 0.5) / scale * SCALE
    item[16:32, :] = direction
    pl.semaphore_wait(barrier, npl - 1 + 2 * quarter)

    def give(src, position, target):
        pltpu.make_async_remote_copy(
            src_ref=src, dst_ref=items.at[position], send_sem=send_sem.at[0], recv_sem=item_sem.at[position],
            device_id=target, device_id_type=MESH,
        ).start()

    def at_other_core(position):
        return half_np + rem(position + (half_np - 1) * core, half_np)

    shifts = [d for p in pairs for d in p] + [half_shift, single]
    slot_of = {d: i for i, d in enumerate(shifts)}

    def give_z(src, d, target):
        i = slot_of[d]
        pltpu.make_async_remote_copy(
            src_ref=src, dst_ref=zitems.at[i], send_sem=send_sem.at[1], recv_sem=recv_sem.at[16 + i],
            device_id=target, device_id_type=MESH,
        ).start()

    send(15, item, hub_item, in_column(quarter))
    for d in sorted((d for d in shifts if d > 0), key=lambda d: d not in pairs[0]):
        give_z(item, d, in_column(-d))
    give(item, at_other_core(0), other_core())
    loop(1, half_np, lambda m: give(item, m, in_plane(2 * m)))

    factor = factor_ref[...]
    gram = lax.dot_general(factor, factor, NT, precision=highest, preferred_element_type=F32)
    g_rows, per = 128 // npl, max(probes // npl, 1)
    proj = lax.dot_general(residual, factor, NT, precision=highest, preferred_element_type=F32)
    g_pad = g_send.shape[1] - g_rows - per
    for i in range(npl):
        g_send[i, 0:g_rows, :] = gram[i * g_rows : i * g_rows + g_rows]
        if i * per < probes:
            g_send[i, g_rows : g_rows + per, :] = proj[i * per : i * per + per]
        else:
            g_send[i, g_rows : g_rows + per, :] = jnp.zeros((per, 128), F32)
        g_send[i, g_rows + per :, :] = jnp.zeros((g_pad, 128), F32)
    loop(1, npl, lambda j: send(2, g_send.at[rem(s + j, npl)], g_rx.at[j], in_plane(j)))

    def pieces(item_val):
        u, d = item_val[0:16], item_val[16:32]
        sq = jnp.sum(u * u, axis=0, keepdims=True)
        return split3(u), [v.astype(F32) for v in split3(sq)], split2(d)

    def tail(sq, first):
        out = jnp.zeros((16, 128), F32)
        for i in range(3):
            out = jnp.where(sub16 == first + i, sq[i], out)
        return jnp.where((sub16 >= 3 - first) & (sub16 < 6 - first), 1.0, out)

    def build_a(slot, item_val):
        (hi, mid, lo), sq, (dhi, dlo) = pieces(item_val)
        at = lanes(slot * 128, 128)
        for g, v in enumerate((hi, hi, mid, hi, lo, mid, tail(sq, 0).astype(BF16))):
            a_mat[g * 16 : g * 16 + 16, at] = v
        a_mat[112:128, at] = jnp.zeros((16, 128), BF16)
        dp[0:16, at] = dhi
        dp[16:32, at] = dlo

    def build_b(item_val):
        (hi, mid, lo), sq, (dhi, dlo) = pieces(item_val)
        hi, mid, lo = (-2.0 * v.astype(F32) for v in (hi, mid, lo))
        wide = jnp.concatenate([hi, mid, hi, lo, hi, mid, tail(sq, 3), jnp.zeros((16, 128), F32)], axis=0)
        return wide.T.astype(BF16), jnp.concatenate([dhi, dlo], axis=0)

    own = item[...]
    build_a(0, own)
    build_a(npl, own)
    b, d_b = build_b(own)
    bt[1, 0:128, :] = b
    dq[1, :, 0:128] = d_b
    right[...] = jnp.zeros_like(right)
    right_f[...] = jnp.zeros_like(right_f)
    left[1] = jnp.zeros(left.shape[1:], F32)

    def take_z(d, store):
        i = slot_of[d]
        wait(recv_sem, 16 + i, zitems.at[i])
        store(build_b(zitems[i]))

    def into(qt, half):
        def store(bd):
            bt[qt, half * 128 : half * 128 + 128, :] = bd[0]
            dq[qt, :, half * 128 : half * 128 + 128] = bd[1]

        return store

    def into_f(bd):
        btf[...] = bd[0]
        dqf[...] = bd[1]

    def prepare(k):
        for i in range(2):
            position = 2 * k + i
            if isinstance(position, int) and position == 0:
                continue
            here = items.at[position]
            pltpu.make_async_copy(here, here, item_sem.at[position]).wait()
            yield position

    def prepare_even(k):
        for position in prepare(k):
            give(items.at[position], at_other_core(position), other_core())
            build_a(position, items[position])

    def prepare_odd(k):
        for position in prepare(k):
            build_a(position, items[position])

    def place(k):
        kk = k + (tp // 2) * div(k + 64 - 3 * tp // 2, 64)
        qt, r = div(kk, tp), rem(kk, tp)
        is_half = div(qt + 2, 3) * div(4 - qt, 3)
        return qt, r + is_half * (tp // 4) * div(r, tp // 4)

    bufs = ((t_a, h_a, l_a), (t_b, h_b, l_b))

    def cross(k, par):
        qt, pt = place(k)
        bufs[par][0][...] = dot(bt[qt], a_mat[:, lanes(pt * 256, 256)])

    def elementwise(par):
        t, h, l = bufs[par]
        h[...], l[...] = split2(matern(t[...]))

    def apply(k, par):
        qt, pt = place(k)
        _, h, l = bufs[par]
        at = lanes(pt * 256, 256)
        d_q, d_p = dq[qt], dp[:, at]
        hi, lo = h[...], l[...]
        left[qt, :, at] = dot(d_q, hi) + dot(d_q, lo)
        right[qt] += dot_nt(d_p, hi) + dot_nt(d_p, lo)

    def steps(first, last, prepared=None):
        def one(k, par):
            if prepared:
                prepared(k)
            apply(k - 2, par)
            elementwise(1 - par)
            cross(k, par)

        k = first
        if first == 0:
            prepared(0)
            cross(0, 0)
            prepared(1)
            elementwise(0)
            cross(1, 1)
            k = 2
        if k % 8 == 0 and (last - k) % 8 == 0:

            def eight(i):
                for n in range(8):
                    one(8 * i + n, n % 2)

            loop(k // 8, last // 8, eight)
        else:
            for kk in range(k, last):
                one(kk, kk % 2)

    def send_right(qt, halves):
        both = right[qt, 0:16, :] + right[qt, 16:32, :]
        for h, d in halves:
            i = slot_of[d]
            rsend[i] = both[:, h * 128 : h * 128 + 128]
            if d > 0:
                send(3, rsend.at[i], rrx.at[d - 1], in_column(d))
            else:
                send(11, rsend.at[i], hub_rx.at[-d - quarter - 1], in_column(d + quarter))

    def window(kind, src, rx):
        loop(1, quarter + 1, lambda i: send(kind, src, rx.at[i - 1], in_column(i)))
        loop(1, quarter, lambda i: send(kind, src, rx.at[quarter - 1 + i], in_column(-i)))

    def window_sum(kind, own, rx):
        wait(recv_sem, kind, rx)
        total = own
        for i in range(2 * quarter - 1):
            total = total + rx[i]
        return total

    def both_windows(kind, src, rx):
        send(kind, src, rx.at[0], in_column(quarter))
        send(kind, src, rx.at[1], in_column(-quarter))

    def gram_stage(stage):
        if stage == 0:
            wait(recv_sem, 2, g_rx.at[pl.ds(1, npl - 1)])
            total = g_send[s]
            for j in range(1, npl):
                total = total + g_rx[j]
            g_piece[...] = total
            window(4, g_piece, g_zx)
        elif stage == 1:
            g_window[...] = window_sum(4, g_piece[...], g_zx)
            both_windows(13, g_window, g_zy)
        elif stage == 2:
            wait(recv_sem, 13, g_zy)
            total = g_zy[0] + g_zy[1]
            g_tot[...] = total
            g_all[s] = total
            loop(1, npl, lambda j: send(5, g_tot, g_all.at[s], in_plane(j)))
        else:
            wait(recv_sem, 5, g_rx.at[pl.ds(1, npl - 1)])
            eye = lax.broadcasted_iota(jnp.int32, (128, 128), 0) == lax.broadcasted_iota(jnp.int32, (128, 128), 1)
            gram = jnp.concatenate([g_all[i, 0:g_rows, :] for i in range(npl)], axis=0)
            core_ref[...] = gram + jnp.where(eye, noise, 0.0)

    lane128 = lax.broadcasted_iota(jnp.int32, (128, 128), 1)
    sub128 = lax.broadcasted_iota(jnp.int32, (128, 128), 0)

    def sweep(k):
        m = core_ref[...]
        line = core_ref[pl.ds(k, 1), :]
        column = jnp.sum(jnp.where(lane128 == k, m, 0.0), axis=1, keepdims=True)
        pivot = jnp.sum(jnp.where(lane128[0:1] == k, line, 0.0), axis=1, keepdims=True)
        inv = 1.0 / pivot
        line = line * inv
        new = jnp.where(sub128 == k, line, m - column * line)
        core_ref[...] = jnp.where(lane128 == k, jnp.where(sub128 == k, -inv, column * inv), new)

    take_z(pairs[0][0], into(0, 0))
    if pairs[0][1] > 0:
        take_z(pairs[0][1], into(0, 1))
    wait(recv_sem, 15, hub_item)
    for d in sorted((d for d in shifts if d < 0), key=lambda d: (d not in pairs[0], d)):
        give_z(hub_item, d, in_column(-d - quarter))
    if pairs[0][1] < 0:
        take_z(pairs[0][1], into(0, 1))
    steps(0, tp // 2, prepare_even)
    gram_stage(0)
    steps(tp // 2, tp, prepare_odd)
    take_z(half_shift, into(1, 1))
    end = tp + tp // 2
    steps(tp, end)
    send_right(0, ((0, pairs[0][0]), (1, pairs[0][1])))
    middle = lanes(npl // 4 * 128, 128)
    hi, lo = split2(matern(dot(bt[1], a_mat[:, middle])))
    d_p = dp[:, middle]
    right[1] += dot_nt(d_p, hi) + dot_nt(d_p, lo)
    for n, pair in enumerate(pairs[1:]):
        take_z(pair[0], into(2 + n, 0))
        take_z(pair[1], into(2 + n, 1))
        steps(end, end + tp // 2)
        if n == 0:
            send_right(1, ((1, half_shift),))
        else:
            send_right(1 + n, ((0, pairs[n][0]), (1, pairs[n][1])))
        gram_stage(1 + n)
        steps(end + tp // 2, end + tp)
        end += tp
    take_z(single, into_f)
    elementwise((end - 1) % 2)
    apply(end - 2, end % 2)
    apply(end - 1, (end - 1) % 2)
    if len(pairs) > 1:
        send_right(len(pairs), ((0, pairs[-1][0]), (1, pairs[-1][1])))
    else:
        send_right(1, ((1, half_shift),))
        gram_stage(1)
        gram_stage(2)

    fbufs = ((ft_a, fh_a, fl_a), (ft_b, fh_b, fl_b))

    def f_cross(k, par):
        fbufs[par][0][...] = dot(btf[...], a_mat[:, lanes(k * 512 + 128, 512)])

    def f_elementwise(par):
        t, h, l = fbufs[par]
        h[...], l[...] = split2(matern(t[...]))

    def f_apply(k, par, last=False):
        _, h, l = fbufs[par]
        d_q, d_p = dqf[...], dp[:, lanes(k * 512 + 128, 512)]
        hi, lo = h[...], l[...]
        out = dot(d_q, hi) + dot(d_q, lo)
        right_f[...] += dot_nt(d_p, hi) + dot_nt(d_p, lo)
        for i in range(4):
            j = k * 4 + 1 + i
            mine = last and i == 3
            total = out[0:16, i * 128 : i * 128 + 128] + out[16:32, i * 128 : i * 128 + 128]
            at = slice(0, 128) if mine else lanes(j * 128, 128)
            for qt in range(left.shape[0]):
                if not (mine and qt == 1) and not (qt == 0 and not pairs):
                    total = total + (left[qt, 0:16, at] + left[qt, 16:32, at])
            lsend[j] = total
            if not mine:
                slot = 2 * rem(j, half_np) + div(j, half_np)
                send(6, lsend.at[j], lrx.at[npl - slot], in_plane(-slot))

    count = npl // 4

    def f_one(k, par):
        f_apply(k - 2, par)
        f_elementwise(1 - par)
        f_cross(k, par)

    f_cross(0, 0)
    f_elementwise(0)
    if count > 1:
        f_cross(1, 1)

        def f_two(i):
            f_one(2 * i, 0)
            f_one(2 * i + 1, 1)

        loop(1, count // 2, f_two)
        f_elementwise((count - 1) % 2)
        f_apply(count - 2, count % 2)
    f_apply(count - 1, (count - 1) % 2, last=True)
    i = slot_of[single]
    rsend[i] = right_f[0:16, :] + right_f[16:32, :]
    send(3, rsend.at[i], rrx.at[single - 1], in_column(single))
    wait(recv_sem, 11, hub_rx)
    total = hub_rx[0]
    for i in range(1, quarter):
        total = total + hub_rx[i]
    hub_out[...] = total
    send(12, hub_out, hub_in, in_column(-quarter))
    gram_stage(3)
    loop(0, 16, sweep)

    wait(recv_sem, 6, lrx.at[pl.ds(1, npl - 1)])
    wait(recv_sem, 3, rrx)
    total = lsend[npl] + (right[1, 0:16, 0:128] + right[1, 16:32, 0:128])
    for j in range(1, npl):
        total = total + lrx[j]
    for i in range(quarter):
        total = total + rrx[i]
    wait(recv_sem, 12, hub_in)
    total = total + hub_in[...]
    image = (var_ref[0] * POLY) * total + noise * direction

    proj_im = lax.dot_general(image, factor, NT, precision=highest, preferred_element_type=F32)
    products = ((direction, image), (residual, image), (image, image), (residual, residual))
    scalars = jnp.zeros((16, 128), F32)
    for n, (a, b) in enumerate(products):
        scalars = jnp.where(lane16 == rem(sub16, 8) * 4 + n, jnp.sum(a * b, axis=1, keepdims=True), scalars)

    def half_of(c):
        first = c == 0
        rows = jnp.where(first, proj_im[0:8], proj_im[8:16])
        inner = jnp.where(first, scalars[0:8], scalars[8:16])
        return rows, jnp.sum(inner, axis=0, keepdims=True)

    for ref, (rows, inner) in ((v_give, half_of(1 - core)), (v_chip, half_of(core))):
        for p in range(8):
            ref[p] = rows[p : p + 1]
        ref[8] = inner
    send(7, v_give, v_take, other_core())
    wait(recv_sem, 7, v_take)
    v_chip[...] += v_take[...]
    loop(1, half_np, lambda m: send(8, v_chip, v_px.at[m], in_plane(2 * m)))
    loop(16, 60, sweep)
    wait(recv_sem, 8, v_px.at[pl.ds(1, half_np - 1)])
    total = v_chip[...]
    for m in range(1, half_np):
        total = total + v_px[m]
    v_plane[...] = total
    window(9, v_plane, v_zx)
    loop(60, 96, sweep)
    v_window[...] = window_sum(9, v_plane[...], v_zx)
    both_windows(14, v_window, v_zy)
    loop(96, 128, sweep)
    wait(recv_sem, 14, v_zy)
    total = v_zy[0] + v_zy[1]
    v_mine[...] = total
    v_all[core] = total
    send(10, v_mine, v_all.at[core], other_core())
    core_inv = -core_ref[...]
    proj_re = jnp.zeros((16, 128), F32)
    for p in range(probes):
        at = g_rows + p % per
        proj_re = jnp.where(sub16 == p, g_all[p // per, at : at + 1, :], proj_re)
    wait(recv_sem, 10, v_take)
    proj_im = jnp.zeros((16, 128), F32)
    for p in range(probes):
        proj_im = jnp.where(sub16 == p, v_all[p // 8, p % 8], proj_im)
    inner = jnp.where(sub16 < 8, v_all[0, 8], v_all[1, 8])
    d_im, r_im, im_im, r_r = (
        jnp.sum(jnp.where(lane16 == rem(sub16, 8) * 4 + n, inner, 0.0), axis=1, keepdims=True) for n in range(4)
    )
    both = jnp.dot(
        jnp.concatenate([proj_re, proj_im], axis=0), core_inv, precision=highest, preferred_element_type=F32
    )
    coef_re, coef_im = both[0:16], both[16:32]
    res_z = (r_r - jnp.sum(proj_re * coef_re, axis=1, keepdims=True)) / noise
    alpha = res_z / d_im
    coef_new = coef_re - alpha * coef_im
    proj_new = proj_re - alpha * proj_im
    new_sq = r_r - 2.0 * alpha * r_im + alpha * alpha * im_im
    res_z_new = (new_sq - jnp.sum(proj_new * coef_new, axis=1, keepdims=True)) / noise
    beta = res_z_new / res_z
    new_residual = residual - alpha * image
    sol_out[...] = solution_ref[...] + alpha * direction
    res_out[...] = new_residual
    fitted = jnp.dot(coef_new, factor, precision=highest, preferred_element_type=F32)
    dir_out[...] = (new_residual - fitted) / noise + beta * direction

    wait(send_sem, 0, items.at[pl.ds(1, npl - 1)])
    wait(send_sem, 1, zitems)
    wait(send_sem, 2, g_rx.at[pl.ds(1, npl - 1)])
    wait(send_sem, 3, rrx)
    wait(send_sem, 4, g_zx)
    wait(send_sem, 5, g_rx.at[pl.ds(1, npl - 1)])
    wait(send_sem, 6, lrx.at[pl.ds(1, npl - 1)])
    wait(send_sem, 7, v_take)
    wait(send_sem, 8, v_px.at[pl.ds(1, half_np - 1)])
    wait(send_sem, 9, v_zx)
    wait(send_sem, 10, v_take)
    wait(send_sem, 11, hub_rx)
    wait(send_sem, 12, hub_in)
    wait(send_sem, 13, g_zy)
    wait(send_sem, 14, v_zy)
    wait(send_sem, 15, hub_item)


def hand_out(*refs):
    for src, dst in zip(refs[:3], refs[3:]):
        dst[...] = src[...]


def local(points, lengthscales, variances, factor, solution, residual, direction):
    nz, npl = Z_HI * Z_LO, X * Y * 2
    quarter = nz // 4
    blocks, nq = 2 * quarter, quarter
    gr, vr = -(-(128 // npl + max(16 // npl, 1)) // 8) * 8, (9, 1, 128)
    wide = (npl + 1) * 128
    vmem = pl.BlockSpec(memory_space=pltpu.VMEM)
    held = [pltpu.VMEM, pltpu.SMEM, pltpu.SMEM, pltpu.VMEM, pltpu.VMEM, pltpu.VMEM, pltpu.VMEM]
    args = (points, lengthscales, variances, factor, solution, residual, direction)
    tile, ftile = (256, 256), (128, 512)
    scratch = [
        ((32, 128), F32), ((npl, 32, 128), F32), ((blocks, 32, 128), F32), ((32, 128), F32),
        ((128, wide), BF16), ((32, wide), BF16), ((nq, 256, 128), BF16), ((nq, 32, 256), BF16),
        ((128, 128), BF16), ((32, 128), BF16),
        (tile, F32), (tile, F32), (tile, BF16), (tile, BF16), (tile, BF16), (tile, BF16),
        (ftile, F32), (ftile, F32), (ftile, BF16), (ftile, BF16), (ftile, BF16), (ftile, BF16),
        ((nq, 32, npl * 128), F32), ((nq, 32, 256), F32), ((32, 128), F32),
        ((npl + 1, 16, 128), F32), ((npl, 16, 128), F32), ((blocks, 16, 128), F32), ((quarter, 16, 128), F32),
        ((quarter, 16, 128), F32), ((16, 128), F32), ((16, 128), F32),
        ((npl, gr, 128), F32), ((npl, gr, 128), F32), ((gr, 128), F32), ((blocks - 1, gr, 128), F32),
        ((gr, 128), F32), ((2, gr, 128), F32),
        ((gr, 128), F32), ((npl, gr, 128), F32), ((128, 128), F32),
        (vr, F32), (vr, F32), (vr, F32), ((npl // 2, *vr), F32), (vr, F32), ((blocks - 1, *vr), F32), (vr, F32),
        ((2, *vr), F32), (vr, F32), ((2, *vr), F32),
    ]
    out = jax.ShapeDtypeStruct(direction.shape, F32)
    outs = pl.pallas_call(
        kernel,
        out_shape=(out, out, out),
        in_specs=[pl.BlockSpec(memory_space=pl.ANY)] * len(args),
        out_specs=(vmem, vmem, vmem),
        scratch_shapes=[space(a.shape, F32) for space, a in zip(held, args)]
        + [pltpu.VMEM(shape, dtype) for shape, dtype in scratch]
        + [pltpu.SemaphoreType.DMA((n,)) for n in (len(args), 16, 16 + blocks, npl)],
        compiler_params=pltpu.CompilerParams(
            collective_id=0, has_side_effects=True, vmem_limit_bytes=56 * 2**20
        ),
    )(*args)
    return pl.pallas_call(
        hand_out,
        out_shape=(out, out, out),
        in_specs=[vmem] * 3,
        out_specs=(vmem, vmem, vmem),
    )(*outs)


def solution(mesh):
    placed = P(None, ("row", "col"))
    return jax.shard_map(
        local,
        mesh=mesh,
        in_specs=(placed, P(), P(), placed, placed, placed, placed),
        out_specs=(placed, placed, placed),
        check_vma=False,
    )
```

```python
import functools
import math

import jax
import jax.numpy as jnp
from jax import lax
from jax.experimental import pallas as pl
from jax.experimental.pallas import tpu as pltpu
from jax.sharding import PartitionSpec as P

F32 = jnp.float32
BF16 = jnp.bfloat16
MESH = pl.DeviceIdType.MESH
highest = lax.Precision.HIGHEST
NT = (((1,), (1,)), ((), ()))
X, Y, Z_HI, Z_LO = 4, 4, 4, 4
LN2 = math.log(2.0)
SCALE = math.sqrt(5.0) / LN2
POLY = LN2 * LN2 / 3.0
POLY_A = 3.0 / LN2
POLY_B = 3.0 / (LN2 * LN2)


def div(a, b):
    return a // b if isinstance(a, int) else lax.div(a, jnp.int32(b))


def rem(a, b):
    return a % b if isinstance(a, int) else lax.rem(a, jnp.int32(b))


def lanes(start, size):
    if isinstance(start, int):
        return slice(start, start + size)
    return pl.ds(pl.multiple_of(start, 128), size)


def split2(v):
    hi = v.astype(BF16)
    return hi, (v - hi.astype(F32)).astype(BF16)


def split3(v):
    hi = v.astype(BF16)
    left = v - hi.astype(F32)
    mid = left.astype(BF16)
    return hi, mid, (left - mid.astype(F32)).astype(BF16)


def matern(t_sq):
    t_sq = jnp.maximum(t_sq, 1e-30)
    t = t_sq * lax.rsqrt(t_sq)
    return (t * (t + POLY_A) + POLY_B) * jnp.exp2(-t)


def dot(a, b):
    return jnp.dot(a, b, preferred_element_type=F32)


def dot_nt(a, b):
    return lax.dot_general(a, b, NT, preferred_element_type=F32)


PLANES = {16: (((2, 3), (-6, -7), (-5, 4)), -8, 1), 8: (((2, -3),), -4, 1)}


def kernel(
    points_hbm, ls_hbm, var_hbm, factor_hbm, solution_hbm, residual_hbm, direction_hbm,
    sol_out, res_out, dir_out,
    points_ref, ls_ref, var_ref, factor_ref, solution_ref, residual_ref, direction_ref,
    item, items, zitems, hub_item, a_mat, dp, bt, dq, btf, dqf,
    t_a, t_b, h_a, h_b, l_a, l_b, ft_a, ft_b, fh_a, fh_b, fl_a, fl_b,
    left, right, right_f, lsend, lrx, rsend, rrx, hub_rx, hub_out, hub_in,
    g_send, g_rx, g_piece, g_zx, g_window, g_zy, g_tot, g_all, core_ref,
    v_give, v_take, v_chip, v_px, v_plane, v_zx, v_window, v_zy, v_all,
    in_sem, send_sem, recv_sem, item_sem,
):
    nz, npl = Z_HI * Z_LO, X * Y * 2
    tp = npl // 2
    pairs, half_shift, single = PLANES[nz]
    quarter = nz // 4
    probes = direction_hbm.shape[0]
    half_np = npl // 2
    row, col = lax.axis_index("row"), lax.axis_index("col")
    z = rem(div(col, 2), Z_HI) * Z_LO + div(row, Y)
    core = rem(col, 2)
    s = (div(col, 2 * Z_HI) * Y + rem(row, Y)) * 2 + core

    def device(zz, ss):
        r = rem(zz, Z_LO) * Y + rem(div(ss, 2), Y)
        c = div(ss, 2 * Y) * (2 * Z_HI) + div(zz, Z_LO) * 2 + rem(ss, 2)
        return (r, c)

    def in_plane(j):
        return device(z, rem(s + j + npl, npl))

    def other_core():
        return device(z, s + 1 - 2 * core)

    def in_column(i, other=0):
        return device(rem(z + i + nz, nz), s + other * (1 - 2 * core))

    def send(kind, src, dst, target):
        pltpu.make_async_remote_copy(
            src_ref=src, dst_ref=dst, send_sem=send_sem.at[kind], recv_sem=recv_sem.at[kind],
            device_id=target, device_id_type=MESH,
        ).start()

    def wait(sem, kind, ref):
        pltpu.make_async_copy(ref, ref, sem.at[kind]).wait()

    def loop(lo, hi, body):
        def step(i, carry):
            body(i)
            return carry

        lax.fori_loop(lo, hi, step, 0)

    loads = [
        pltpu.make_async_copy(src, dst, in_sem.at[i])
        for i, (src, dst) in enumerate((
            (ls_hbm, ls_ref), (var_hbm, var_ref), (points_hbm, points_ref), (direction_hbm, direction_ref),
            (factor_hbm, factor_ref), (residual_hbm, residual_ref), (solution_hbm, solution_ref),
        ))
    ]
    for load in loads:
        load.start()
    barrier = pltpu.get_barrier_semaphore()
    loop(1, npl, lambda j: pl.semaphore_signal(barrier, inc=1, device_id=in_plane(j), device_id_type=MESH))
    for sign in (1, -1):
        far = in_column(sign * quarter, 1)
        pl.semaphore_signal(barrier, inc=1, device_id=far, device_id_type=MESH)
        loop(
            1,
            quarter + 1,
            lambda i, sign=sign: pl.semaphore_signal(
                barrier, inc=1, device_id=in_column(sign * i), device_id_type=MESH
            ),
        )

    for load in loads[:4]:
        load.wait()

    sub16 = lax.broadcasted_iota(jnp.int32, (16, 128), 0)
    lane16 = lax.broadcasted_iota(jnp.int32, (16, 128), 1)
    scale = jnp.zeros((16, 128), F32)
    for i in range(16):
        scale = jnp.where(sub16 == i, ls_ref[i], scale)
    direction = direction_ref[...]
    noise = var_ref[1]
    item[0:16, :] = (points_ref[...] - 0.5) / scale * SCALE
    item[16:32, :] = direction
    pl.semaphore_wait(barrier, npl - 1 + 2 * quarter + 2)

    def give(src, position, target):
        pltpu.make_async_remote_copy(
            src_ref=src, dst_ref=items.at[position], send_sem=send_sem.at[0], recv_sem=item_sem.at[position],
            device_id=target, device_id_type=MESH,
        ).start()

    def at_other_core(position):
        return half_np + rem(position + (half_np - 1) * core, half_np)

    shifts = [d for p in pairs for d in p] + [half_shift, single]
    slot_of = {d: i for i, d in enumerate(shifts)}

    def give_z(src, d, target):
        i = slot_of[d]
        pltpu.make_async_remote_copy(
            src_ref=src, dst_ref=zitems.at[i], send_sem=send_sem.at[1], recv_sem=recv_sem.at[16 + i],
            device_id=target, device_id_type=MESH,
        ).start()

    send(15, item, hub_item, in_column(quarter))
    for d in sorted((d for d in shifts if d > 0), key=lambda d: d not in pairs[0]):
        give_z(item, d, in_column(-d))
    give(item, at_other_core(0), other_core())
    loop(1, half_np, lambda m: give(item, m, in_plane(2 * m)))

    for load in loads[4:]:
        load.wait()
    residual = residual_ref[...]
    factor = factor_ref[...]
    gram = lax.dot_general(factor, factor, NT, precision=highest, preferred_element_type=F32)
    g_rows, per = 128 // npl, max(probes // npl, 1)
    proj = lax.dot_general(residual, factor, NT, precision=highest, preferred_element_type=F32)
    g_pad = g_send.shape[1] - g_rows - per
    for i in range(npl):
        g_send[i, 0:g_rows, :] = gram[i * g_rows : i * g_rows + g_rows]
        if i * per < probes:
            g_send[i, g_rows : g_rows + per, :] = proj[i * per : i * per + per]
        else:
            g_send[i, g_rows : g_rows + per, :] = jnp.zeros((per, 128), F32)
        g_send[i, g_rows + per :, :] = jnp.zeros((g_pad, 128), F32)
    loop(1, npl, lambda j: send(2, g_send.at[rem(s + j, npl)], g_rx.at[j], in_plane(j)))

    def pieces(item_val):
        u, d = item_val[0:16], item_val[16:32]
        sq = jnp.sum(u * u, axis=0, keepdims=True)
        return split3(u), [v.astype(F32) for v in split3(sq)], split2(d)

    def tail(sq, first):
        out = jnp.zeros((16, 128), F32)
        for i in range(3):
            out = jnp.where(sub16 == first + i, sq[i], out)
        return jnp.where((sub16 >= 3 - first) & (sub16 < 6 - first), 1.0, out)

    def build_a(slot, item_val):
        (hi, mid, lo), sq, (dhi, dlo) = pieces(item_val)
        at = lanes(slot * 128, 128)
        for g, v in enumerate((hi, hi, mid, hi, lo, mid, tail(sq, 0).astype(BF16))):
            a_mat[g * 16 : g * 16 + 16, at] = v
        a_mat[112:128, at] = jnp.zeros((16, 128), BF16)
        dp[0:16, at] = dhi
        dp[16:32, at] = dlo

    def build_b(item_val):
        (hi, mid, lo), sq, (dhi, dlo) = pieces(item_val)
        hi, mid, lo = (-2.0 * v.astype(F32) for v in (hi, mid, lo))
        wide = jnp.concatenate([hi, mid, hi, lo, hi, mid, tail(sq, 3), jnp.zeros((16, 128), F32)], axis=0)
        return wide.T.astype(BF16), jnp.concatenate([dhi, dlo], axis=0)

    own = item[...]
    build_a(0, own)
    build_a(npl, own)
    b, d_b = build_b(own)
    bt[1, 0:128, :] = b
    dq[1, :, 0:128] = d_b
    right[...] = jnp.zeros_like(right)
    right_f[...] = jnp.zeros_like(right_f)
    left[1] = jnp.zeros(left.shape[1:], F32)

    def take_z(d, store):
        i = slot_of[d]
        wait(recv_sem, 16 + i, zitems.at[i])
        store(build_b(zitems[i]))

    def into(qt, half):
        def store(bd):
            bt[qt, half * 128 : half * 128 + 128, :] = bd[0]
            dq[qt, :, half * 128 : half * 128 + 128] = bd[1]

        return store

    def into_f(bd):
        btf[...] = bd[0]
        dqf[...] = bd[1]

    def prepare(k):
        for i in range(2):
            position = 2 * k + i
            if isinstance(position, int) and position == 0:
                continue
            here = items.at[position]
            pltpu.make_async_copy(here, here, item_sem.at[position]).wait()
            yield position

    def prepare_even(k):
        for position in prepare(k):
            give(items.at[position], at_other_core(position), other_core())
            build_a(position, items[position])

    def prepare_odd(k):
        for position in prepare(k):
            build_a(position, items[position])

    def place(k):
        kk = k + (tp // 2) * div(k + 64 - 3 * tp // 2, 64)
        qt, r = div(kk, tp), rem(kk, tp)
        is_half = div(qt + 2, 3) * div(4 - qt, 3)
        return qt, r + is_half * (tp // 4) * div(r, tp // 4)

    bufs = ((t_a, h_a, l_a), (t_b, h_b, l_b))

    def cross(k, par):
        qt, pt = place(k)
        bufs[par][0][...] = dot(bt[qt], a_mat[:, lanes(pt * 256, 256)])

    def elementwise(par):
        t, h, l = bufs[par]
        h[...], l[...] = split2(matern(t[...]))

    def apply(k, par):
        qt, pt = place(k)
        _, h, l = bufs[par]
        at = lanes(pt * 256, 256)
        d_q, d_p = dq[qt], dp[:, at]
        hi, lo = h[...], l[...]
        left[qt, :, at] = dot(d_q, hi) + dot(d_q, lo)
        right[qt] += dot_nt(d_p, hi) + dot_nt(d_p, lo)

    def steps(first, last, prepared=None):
        def one(k, par):
            if prepared:
                prepared(k)
            apply(k - 2, par)
            elementwise(1 - par)
            cross(k, par)

        k = first
        if first == 0:
            prepared(0)
            cross(0, 0)
            prepared(1)
            elementwise(0)
            cross(1, 1)
            k = 2
        if k % 8 == 0 and (last - k) % 8 == 0:

            def eight(i):
                for n in range(8):
                    one(8 * i + n, n % 2)

            loop(k // 8, last // 8, eight)
        else:
            for kk in range(k, last):
                one(kk, kk % 2)

    def send_right(qt, halves):
        both = right[qt, 0:16, :] + right[qt, 16:32, :]
        for h, d in halves:
            i = slot_of[d]
            rsend[i] = both[:, h * 128 : h * 128 + 128]
            if d > 0:
                send(3, rsend.at[i], rrx.at[d - 1], in_column(d))
            else:
                send(11, rsend.at[i], hub_rx.at[-d - quarter - 1], in_column(d + quarter))

    def window(kind, src, rx):
        loop(1, quarter + 1, lambda i: send(kind, src, rx.at[i - 1], in_column(i)))
        loop(1, quarter, lambda i: send(kind, src, rx.at[quarter - 1 + i], in_column(-i)))

    def window_sum(kind, own, rx):
        wait(recv_sem, kind, rx)
        total = own
        for i in range(2 * quarter - 1):
            total = total + rx[i]
        return total

    def both_windows(kind, src, rx):
        send(kind, src, rx.at[0], in_column(quarter))
        send(kind, src, rx.at[1], in_column(-quarter))

    def gram_stage(stage):
        if stage == 0:
            wait(recv_sem, 2, g_rx.at[pl.ds(1, npl - 1)])
            total = g_send[s]
            for j in range(1, npl):
                total = total + g_rx[j]
            g_piece[...] = total
            window(4, g_piece, g_zx)
        elif stage == 1:
            g_window[...] = window_sum(4, g_piece[...], g_zx)
            both_windows(13, g_window, g_zy)
        elif stage == 2:
            wait(recv_sem, 13, g_zy)
            total = g_zy[0] + g_zy[1]
            g_tot[...] = total
            g_all[s] = total
            loop(1, npl, lambda j: send(5, g_tot, g_all.at[s], in_plane(j)))
        else:
            wait(recv_sem, 5, g_rx.at[pl.ds(1, npl - 1)])
            eye = lax.broadcasted_iota(jnp.int32, (128, 128), 0) == lax.broadcasted_iota(jnp.int32, (128, 128), 1)
            gram = jnp.concatenate([g_all[i, 0:g_rows, :] for i in range(npl)], axis=0)
            core_ref[...] = gram + jnp.where(eye, noise, 0.0)

    lane128 = lax.broadcasted_iota(jnp.int32, (128, 128), 1)
    sub128 = lax.broadcasted_iota(jnp.int32, (128, 128), 0)

    def sweep(k):
        m = core_ref[...]
        line = core_ref[pl.ds(k, 1), :]
        column = jnp.sum(jnp.where(lane128 == k, m, 0.0), axis=1, keepdims=True)
        pivot = jnp.sum(jnp.where(lane128[0:1] == k, line, 0.0), axis=1, keepdims=True)
        inv = 1.0 / pivot
        line = line * inv
        new = jnp.where(sub128 == k, line, m - column * line)
        core_ref[...] = jnp.where(lane128 == k, jnp.where(sub128 == k, -inv, column * inv), new)

    take_z(pairs[0][0], into(0, 0))
    if pairs[0][1] > 0:
        take_z(pairs[0][1], into(0, 1))
    wait(recv_sem, 15, hub_item)
    for d in sorted((d for d in shifts if d < 0), key=lambda d: (d not in pairs[0], d)):
        give_z(hub_item, d, in_column(-d - quarter))
    if pairs[0][1] < 0:
        take_z(pairs[0][1], into(0, 1))
    steps(0, tp // 2, prepare_even)
    gram_stage(0)
    steps(tp // 2, tp, prepare_odd)
    take_z(half_shift, into(1, 1))
    end = tp + tp // 2
    steps(tp, end)
    send_right(0, ((0, pairs[0][0]), (1, pairs[0][1])))
    middle = lanes(npl // 4 * 128, 128)
    hi, lo = split2(matern(dot(bt[1], a_mat[:, middle])))
    d_p = dp[:, middle]
    right[1] += dot_nt(d_p, hi) + dot_nt(d_p, lo)
    for n, pair in enumerate(pairs[1:]):
        take_z(pair[0], into(2 + n, 0))
        take_z(pair[1], into(2 + n, 1))
        steps(end, end + tp // 2)
        if n == 0:
            send_right(1, ((1, half_shift),))
        else:
            send_right(1 + n, ((0, pairs[n][0]), (1, pairs[n][1])))
        gram_stage(1 + n)
        steps(end + tp // 2, end + tp)
        end += tp
    take_z(single, into_f)
    elementwise((end - 1) % 2)
    apply(end - 2, end % 2)
    apply(end - 1, (end - 1) % 2)
    if len(pairs) > 1:
        send_right(len(pairs), ((0, pairs[-1][0]), (1, pairs[-1][1])))
    else:
        send_right(1, ((1, half_shift),))
        gram_stage(1)
        gram_stage(2)

    fbufs = ((ft_a, fh_a, fl_a), (ft_b, fh_b, fl_b))

    def f_cross(k, par):
        fbufs[par][0][...] = dot(btf[...], a_mat[:, lanes(k * 512 + 128, 512)])

    def f_elementwise(par):
        t, h, l = fbufs[par]
        h[...], l[...] = split2(matern(t[...]))

    def f_apply(k, par, last=False):
        _, h, l = fbufs[par]
        d_q, d_p = dqf[...], dp[:, lanes(k * 512 + 128, 512)]
        hi, lo = h[...], l[...]
        out = dot(d_q, hi) + dot(d_q, lo)
        right_f[...] += dot_nt(d_p, hi) + dot_nt(d_p, lo)
        for i in range(4):
            j = k * 4 + 1 + i
            mine = last and i == 3
            total = out[0:16, i * 128 : i * 128 + 128] + out[16:32, i * 128 : i * 128 + 128]
            at = slice(0, 128) if mine else lanes(j * 128, 128)
            for qt in range(left.shape[0]):
                if not (mine and qt == 1) and not (qt == 0 and not pairs):
                    total = total + (left[qt, 0:16, at] + left[qt, 16:32, at])
            lsend[j] = total
            if not mine:
                slot = 2 * rem(j, half_np) + div(j, half_np)
                send(6, lsend.at[j], lrx.at[npl - slot], in_plane(-slot))

    count = npl // 4

    def f_one(k, par):
        f_apply(k - 2, par)
        f_elementwise(1 - par)
        f_cross(k, par)

    f_cross(0, 0)
    f_elementwise(0)
    if count > 1:
        f_cross(1, 1)

        def f_two(i):
            f_one(2 * i, 0)
            f_one(2 * i + 1, 1)

        loop(1, count // 2, f_two)
        f_elementwise((count - 1) % 2)
        f_apply(count - 2, count % 2)
    f_apply(count - 1, (count - 1) % 2, last=True)
    i = slot_of[single]
    rsend[i] = right_f[0:16, :] + right_f[16:32, :]
    send(3, rsend.at[i], rrx.at[single - 1], in_column(single))
    wait(recv_sem, 11, hub_rx)
    total = hub_rx[0]
    for i in range(1, quarter):
        total = total + hub_rx[i]
    hub_out[...] = total
    send(12, hub_out, hub_in, in_column(-quarter))
    gram_stage(3)
    loop(0, 16, sweep)

    wait(recv_sem, 6, lrx.at[pl.ds(1, npl - 1)])
    wait(recv_sem, 3, rrx)
    total = lsend[npl] + (right[1, 0:16, 0:128] + right[1, 16:32, 0:128])
    for j in range(1, npl):
        total = total + lrx[j]
    for i in range(quarter):
        total = total + rrx[i]
    wait(recv_sem, 12, hub_in)
    total = total + hub_in[...]
    image = (var_ref[0] * POLY) * total + noise * direction

    proj_im = lax.dot_general(image, factor, NT, precision=highest, preferred_element_type=F32)
    products = ((direction, image), (residual, image), (image, image), (residual, residual))
    scalars = jnp.zeros((16, 128), F32)
    for n, (a, b) in enumerate(products):
        scalars = jnp.where(lane16 == rem(sub16, 8) * 4 + n, jnp.sum(a * b, axis=1, keepdims=True), scalars)

    def half_of(c):
        first = c == 0
        rows = jnp.where(first, proj_im[0:8], proj_im[8:16])
        inner = jnp.where(first, scalars[0:8], scalars[8:16])
        return rows, jnp.sum(inner, axis=0, keepdims=True)

    for ref, (rows, inner) in ((v_give, half_of(1 - core)), (v_chip, half_of(core))):
        for p in range(8):
            ref[p] = rows[p : p + 1]
        ref[8] = inner
    send(7, v_give, v_take, other_core())
    wait(recv_sem, 7, v_take)
    v_chip[...] += v_take[...]
    loop(1, half_np, lambda m: send(8, v_chip, v_px.at[m], in_plane(2 * m)))
    loop(16, 60, sweep)
    wait(recv_sem, 8, v_px.at[pl.ds(1, half_np - 1)])
    total = v_chip[...]
    for m in range(1, half_np):
        total = total + v_px[m]
    v_plane[...] = total
    window(9, v_plane, v_zx)
    loop(60, 96, sweep)
    v_window[...] = window_sum(9, v_plane[...], v_zx)
    for other in (0, 1):
        send(14, v_window, v_zy.at[core, 0], in_column(quarter, other))
        send(14, v_window, v_zy.at[core, 1], in_column(-quarter, other))
    loop(96, 128, sweep)
    core_inv = -core_ref[...]
    both_inv = jnp.concatenate(
        [core_inv, jnp.dot(core_inv, factor, precision=highest, preferred_element_type=F32)], axis=1
    )
    proj_re = jnp.zeros((16, 128), F32)
    for p in range(probes):
        at = g_rows + p % per
        proj_re = jnp.where(sub16 == p, g_all[p // per, at : at + 1, :], proj_re)
    of_re = jnp.dot(proj_re, both_inv, precision=highest, preferred_element_type=F32)
    wait(recv_sem, 14, v_zy)
    for h in range(2):
        v_all[h] = v_zy[h, 0] + v_zy[h, 1]
    proj_im = jnp.zeros((16, 128), F32)
    for p in range(probes):
        proj_im = jnp.where(sub16 == p, v_all[p // 8, p % 8], proj_im)
    inner = jnp.where(sub16 < 8, v_all[0, 8], v_all[1, 8])
    d_im, r_im, im_im, r_r = (
        jnp.sum(jnp.where(lane16 == rem(sub16, 8) * 4 + n, inner, 0.0), axis=1, keepdims=True) for n in range(4)
    )
    of_im = jnp.dot(proj_im, both_inv, precision=highest, preferred_element_type=F32)
    coef_re, coef_im = of_re[:, 0:128], of_im[:, 0:128]
    res_z = (r_r - jnp.sum(proj_re * coef_re, axis=1, keepdims=True)) / noise
    alpha = res_z / d_im
    coef_new = coef_re - alpha * coef_im
    proj_new = proj_re - alpha * proj_im
    new_sq = r_r - 2.0 * alpha * r_im + alpha * alpha * im_im
    res_z_new = (new_sq - jnp.sum(proj_new * coef_new, axis=1, keepdims=True)) / noise
    beta = res_z_new / res_z
    new_residual = residual - alpha * image
    sol_out[...] = solution_ref[...] + alpha * direction
    res_out[...] = new_residual
    fitted = of_re[:, 128:256] - alpha * of_im[:, 128:256]
    dir_out[...] = (new_residual - fitted) / noise + beta * direction

    wait(send_sem, 0, items.at[pl.ds(1, npl - 1)])
    wait(send_sem, 1, zitems)
    wait(send_sem, 2, g_rx.at[pl.ds(1, npl - 1)])
    wait(send_sem, 3, rrx)
    wait(send_sem, 4, g_zx)
    wait(send_sem, 5, g_rx.at[pl.ds(1, npl - 1)])
    wait(send_sem, 6, lrx.at[pl.ds(1, npl - 1)])
    wait(send_sem, 7, v_take)
    wait(send_sem, 8, v_px.at[pl.ds(1, half_np - 1)])
    wait(send_sem, 9, v_zx)
    wait(send_sem, 11, hub_rx)
    wait(send_sem, 12, hub_in)
    wait(send_sem, 13, g_zy)
    wait(send_sem, 14, v_zy)
    wait(send_sem, 15, hub_item)


def hand_out(*refs):
    for src, dst in zip(refs[:3], refs[3:]):
        dst[...] = src[...]


def local(points, lengthscales, variances, factor, solution, residual, direction):
    nz, npl = Z_HI * Z_LO, X * Y * 2
    quarter = nz // 4
    blocks, nq = 2 * quarter, quarter
    gr, vr = -(-(128 // npl + max(16 // npl, 1)) // 8) * 8, (9, 1, 128)
    wide = (npl + 1) * 128
    vmem = pl.BlockSpec(memory_space=pltpu.VMEM)
    held = [pltpu.VMEM, pltpu.SMEM, pltpu.SMEM, pltpu.VMEM, pltpu.VMEM, pltpu.VMEM, pltpu.VMEM]
    args = (points, lengthscales, variances, factor, solution, residual, direction)
    tile, ftile = (256, 256), (128, 512)
    scratch = [
        ((32, 128), F32), ((npl, 32, 128), F32), ((blocks, 32, 128), F32), ((32, 128), F32),
        ((128, wide), BF16), ((32, wide), BF16), ((nq, 256, 128), BF16), ((nq, 32, 256), BF16),
        ((128, 128), BF16), ((32, 128), BF16),
        (tile, F32), (tile, F32), (tile, BF16), (tile, BF16), (tile, BF16), (tile, BF16),
        (ftile, F32), (ftile, F32), (ftile, BF16), (ftile, BF16), (ftile, BF16), (ftile, BF16),
        ((nq, 32, npl * 128), F32), ((nq, 32, 256), F32), ((32, 128), F32),
        ((npl + 1, 16, 128), F32), ((npl, 16, 128), F32), ((blocks, 16, 128), F32), ((quarter, 16, 128), F32),
        ((quarter, 16, 128), F32), ((16, 128), F32), ((16, 128), F32),
        ((npl, gr, 128), F32), ((npl, gr, 128), F32), ((gr, 128), F32), ((blocks - 1, gr, 128), F32),
        ((gr, 128), F32), ((2, gr, 128), F32),
        ((gr, 128), F32), ((npl, gr, 128), F32), ((128, 128), F32),
        (vr, F32), (vr, F32), (vr, F32), ((npl // 2, *vr), F32), (vr, F32), ((blocks - 1, *vr), F32), (vr, F32),
        ((2, 2, *vr), F32), ((2, *vr), F32),
    ]
    out = jax.ShapeDtypeStruct(direction.shape, F32)
    outs = pl.pallas_call(
        kernel,
        out_shape=(out, out, out),
        in_specs=[pl.BlockSpec(memory_space=pl.ANY)] * len(args),
        out_specs=(vmem, vmem, vmem),
        scratch_shapes=[space(a.shape, F32) for space, a in zip(held, args)]
        + [pltpu.VMEM(shape, dtype) for shape, dtype in scratch]
        + [pltpu.SemaphoreType.DMA((n,)) for n in (len(args), 16, 16 + blocks, npl)],
        compiler_params=pltpu.CompilerParams(
            collective_id=0, has_side_effects=True, vmem_limit_bytes=56 * 2**20
        ),
    )(*args)
    return pl.pallas_call(
        hand_out,
        out_shape=(out, out, out),
        in_specs=[vmem] * 3,
        out_specs=(vmem, vmem, vmem),
    )(*outs)


def solution(mesh):
    placed = P(None, ("row", "col"))
    return jax.shard_map(
        local,
        mesh=mesh,
        in_specs=(placed, P(), P(), placed, placed, placed, placed),
        out_specs=(placed, placed, placed),
        check_vma=False,
    )
```

```python
import functools
import math

import jax
import jax.numpy as jnp
from jax import lax
from jax.experimental import pallas as pl
from jax.experimental.pallas import tpu as pltpu
from jax.sharding import PartitionSpec as P

F32 = jnp.float32
BF16 = jnp.bfloat16
MESH = pl.DeviceIdType.MESH
highest = lax.Precision.HIGHEST
NT = (((1,), (1,)), ((), ()))
X, Y, Z_HI, Z_LO = 4, 4, 4, 4
LN2 = math.log(2.0)
SCALE = math.sqrt(5.0) / LN2
POLY = LN2 * LN2 / 3.0
POLY_A = 3.0 / LN2
POLY_B = 3.0 / (LN2 * LN2)


def div(a, b):
    return a // b if isinstance(a, int) else lax.div(a, jnp.int32(b))


def rem(a, b):
    return a % b if isinstance(a, int) else lax.rem(a, jnp.int32(b))


def lanes(start, size):
    if isinstance(start, int):
        return slice(start, start + size)
    return pl.ds(pl.multiple_of(start, 128), size)


def split2(v):
    hi = v.astype(BF16)
    return hi, (v - hi.astype(F32)).astype(BF16)


def split3(v):
    hi = v.astype(BF16)
    left = v - hi.astype(F32)
    mid = left.astype(BF16)
    return hi, mid, (left - mid.astype(F32)).astype(BF16)


def matern(t_sq):
    t_sq = jnp.maximum(t_sq, 1e-30)
    t = t_sq * lax.rsqrt(t_sq)
    return (t * (t + POLY_A) + POLY_B) * jnp.exp2(-t)


def dot(a, b):
    return jnp.dot(a, b, preferred_element_type=F32)


def dot_nt(a, b):
    return lax.dot_general(a, b, NT, preferred_element_type=F32)


PLANES = {16: (((2, 3), (-6, -7), (-5, 4)), -8, 1), 8: (((2, -3),), -4, 1)}


def kernel(
    points_hbm, ls_hbm, var_hbm, factor_hbm, solution_hbm, residual_hbm, direction_hbm,
    sol_out, res_out, dir_out,
    points_ref, ls_ref, var_ref, factor_ref, solution_ref, residual_ref, direction_ref,
    item, items, zitems, hub_item, a_mat, dp, bt, dq, btf, dqf,
    t_a, t_b, h_a, h_b, l_a, l_b, ft_a, ft_b, fh_a, fh_b, fl_a, fl_b,
    left, right, right_f, lsend, lrx, rsend, rrx, hub_rx, hub_out, hub_in,
    g_send, g_rx, g_piece, g_zx, g_window, g_zy, g_tot, g_all, core_ref,
    v_half, v_px, v_plane, v_zx, v_window, v_zy, v_all,
    in_sem, send_sem, recv_sem, item_sem,
):
    nz, npl = Z_HI * Z_LO, X * Y * 2
    tp = npl // 2
    pairs, half_shift, single = PLANES[nz]
    quarter = nz // 4
    probes = direction_hbm.shape[0]
    half_np = npl // 2
    row, col = lax.axis_index("row"), lax.axis_index("col")
    z = rem(div(col, 2), Z_HI) * Z_LO + div(row, Y)
    core = rem(col, 2)
    s = (div(col, 2 * Z_HI) * Y + rem(row, Y)) * 2 + core

    def device(zz, ss):
        r = rem(zz, Z_LO) * Y + rem(div(ss, 2), Y)
        c = div(ss, 2 * Y) * (2 * Z_HI) + div(zz, Z_LO) * 2 + rem(ss, 2)
        return (r, c)

    def in_plane(j):
        return device(z, rem(s + j + npl, npl))

    def other_core():
        return device(z, s + 1 - 2 * core)

    def in_column(i, other=0):
        return device(rem(z + i + nz, nz), s + other * (1 - 2 * core))

    def send(kind, src, dst, target):
        pltpu.make_async_remote_copy(
            src_ref=src, dst_ref=dst, send_sem=send_sem.at[kind], recv_sem=recv_sem.at[kind],
            device_id=target, device_id_type=MESH,
        ).start()

    def wait(sem, kind, ref):
        pltpu.make_async_copy(ref, ref, sem.at[kind]).wait()

    def loop(lo, hi, body):
        def step(i, carry):
            body(i)
            return carry

        lax.fori_loop(lo, hi, step, 0)

    loads = [
        pltpu.make_async_copy(src, dst, in_sem.at[i])
        for i, (src, dst) in enumerate((
            (ls_hbm, ls_ref), (var_hbm, var_ref), (points_hbm, points_ref), (direction_hbm, direction_ref),
            (factor_hbm, factor_ref), (residual_hbm, residual_ref), (solution_hbm, solution_ref),
        ))
    ]
    for load in loads:
        load.start()
    barrier = pltpu.get_barrier_semaphore()
    loop(1, npl, lambda j: pl.semaphore_signal(barrier, inc=1, device_id=in_plane(j), device_id_type=MESH))
    for sign in (1, -1):
        far = in_column(sign * quarter, 1)
        pl.semaphore_signal(barrier, inc=1, device_id=far, device_id_type=MESH)
        loop(
            1,
            quarter + 1,
            lambda i, sign=sign: pl.semaphore_signal(
                barrier, inc=1, device_id=in_column(sign * i), device_id_type=MESH
            ),
        )

    for load in loads[:4]:
        load.wait()

    sub16 = lax.broadcasted_iota(jnp.int32, (16, 128), 0)
    lane16 = lax.broadcasted_iota(jnp.int32, (16, 128), 1)
    scale = jnp.zeros((16, 128), F32)
    for i in range(16):
        scale = jnp.where(sub16 == i, ls_ref[i], scale)
    direction = direction_ref[...]
    noise = var_ref[1]
    item[0:16, :] = (points_ref[...] - 0.5) / scale * SCALE
    item[16:32, :] = direction
    pl.semaphore_wait(barrier, npl - 1 + 2 * quarter + 2)

    def give(src, position, target):
        pltpu.make_async_remote_copy(
            src_ref=src, dst_ref=items.at[position], send_sem=send_sem.at[0], recv_sem=item_sem.at[position],
            device_id=target, device_id_type=MESH,
        ).start()

    def at_other_core(position):
        return half_np + rem(position + (half_np - 1) * core, half_np)

    shifts = [d for p in pairs for d in p] + [half_shift, single]
    slot_of = {d: i for i, d in enumerate(shifts)}

    def give_z(src, d, target):
        i = slot_of[d]
        pltpu.make_async_remote_copy(
            src_ref=src, dst_ref=zitems.at[i], send_sem=send_sem.at[1], recv_sem=recv_sem.at[16 + i],
            device_id=target, device_id_type=MESH,
        ).start()

    send(15, item, hub_item, in_column(quarter))
    for d in sorted((d for d in shifts if d > 0), key=lambda d: d not in pairs[0]):
        give_z(item, d, in_column(-d))
    give(item, at_other_core(0), other_core())
    loop(1, half_np, lambda m: give(item, m, in_plane(2 * m)))

    for load in loads[4:]:
        load.wait()
    residual = residual_ref[...]
    factor = factor_ref[...]
    gram = lax.dot_general(factor, factor, NT, precision=highest, preferred_element_type=F32)
    g_rows, per = 128 // npl, max(probes // npl, 1)
    proj = lax.dot_general(residual, factor, NT, precision=highest, preferred_element_type=F32)
    g_pad = g_send.shape[1] - g_rows - per
    for i in range(npl):
        g_send[i, 0:g_rows, :] = gram[i * g_rows : i * g_rows + g_rows]
        if i * per < probes:
            g_send[i, g_rows : g_rows + per, :] = proj[i * per : i * per + per]
        else:
            g_send[i, g_rows : g_rows + per, :] = jnp.zeros((per, 128), F32)
        g_send[i, g_rows + per :, :] = jnp.zeros((g_pad, 128), F32)
    loop(1, npl, lambda j: send(2, g_send.at[rem(s + j, npl)], g_rx.at[j], in_plane(j)))

    def pieces(item_val):
        u, d = item_val[0:16], item_val[16:32]
        sq = jnp.sum(u * u, axis=0, keepdims=True)
        return split3(u), [v.astype(F32) for v in split3(sq)], split2(d)

    def tail(sq, first):
        out = jnp.zeros((16, 128), F32)
        for i in range(3):
            out = jnp.where(sub16 == first + i, sq[i], out)
        return jnp.where((sub16 >= 3 - first) & (sub16 < 6 - first), 1.0, out)

    def build_a(slot, item_val):
        (hi, mid, lo), sq, (dhi, dlo) = pieces(item_val)
        at = lanes(slot * 128, 128)
        for g, v in enumerate((hi, hi, mid, hi, lo, mid, tail(sq, 0).astype(BF16))):
            a_mat[g * 16 : g * 16 + 16, at] = v
        a_mat[112:128, at] = jnp.zeros((16, 128), BF16)
        dp[0:16, at] = dhi
        dp[16:32, at] = dlo

    def build_b(item_val):
        (hi, mid, lo), sq, (dhi, dlo) = pieces(item_val)
        hi, mid, lo = (-2.0 * v.astype(F32) for v in (hi, mid, lo))
        wide = jnp.concatenate([hi, mid, hi, lo, hi, mid, tail(sq, 3), jnp.zeros((16, 128), F32)], axis=0)
        return wide.T.astype(BF16), jnp.concatenate([dhi, dlo], axis=0)

    own = item[...]
    build_a(0, own)
    build_a(npl, own)
    b, d_b = build_b(own)
    bt[1, 0:128, :] = b
    dq[1, :, 0:128] = d_b
    right[...] = jnp.zeros_like(right)
    right_f[...] = jnp.zeros_like(right_f)
    left[1] = jnp.zeros(left.shape[1:], F32)

    def take_z(d, store):
        i = slot_of[d]
        wait(recv_sem, 16 + i, zitems.at[i])
        store(build_b(zitems[i]))

    def into(qt, half):
        def store(bd):
            bt[qt, half * 128 : half * 128 + 128, :] = bd[0]
            dq[qt, :, half * 128 : half * 128 + 128] = bd[1]

        return store

    def into_f(bd):
        btf[...] = bd[0]
        dqf[...] = bd[1]

    def prepare(k):
        for i in range(2):
            position = 2 * k + i
            if isinstance(position, int) and position == 0:
                continue
            here = items.at[position]
            pltpu.make_async_copy(here, here, item_sem.at[position]).wait()
            yield position

    def prepare_even(k):
        for position in prepare(k):
            give(items.at[position], at_other_core(position), other_core())
            build_a(position, items[position])

    def prepare_odd(k):
        for position in prepare(k):
            build_a(position, items[position])

    def place(k):
        kk = k + (tp // 2) * div(k + 64 - 3 * tp // 2, 64)
        qt, r = div(kk, tp), rem(kk, tp)
        is_half = div(qt + 2, 3) * div(4 - qt, 3)
        return qt, r + is_half * (tp // 4) * div(r, tp // 4)

    bufs = ((t_a, h_a, l_a), (t_b, h_b, l_b))

    def cross(k, par):
        qt, pt = place(k)
        bufs[par][0][...] = dot(bt[qt], a_mat[:, lanes(pt * 256, 256)])

    def elementwise(par):
        t, h, l = bufs[par]
        h[...], l[...] = split2(matern(t[...]))

    def apply(k, par):
        qt, pt = place(k)
        _, h, l = bufs[par]
        at = lanes(pt * 256, 256)
        d_q, d_p = dq[qt], dp[:, at]
        hi, lo = h[...], l[...]
        left[qt, :, at] = dot(d_q, hi) + dot(d_q, lo)
        right[qt] += dot_nt(d_p, hi) + dot_nt(d_p, lo)

    def steps(first, last, prepared=None):
        def one(k, par):
            if prepared:
                prepared(k)
            apply(k - 2, par)
            elementwise(1 - par)
            cross(k, par)

        k = first
        if first == 0:
            prepared(0)
            cross(0, 0)
            prepared(1)
            elementwise(0)
            cross(1, 1)
            k = 2
        if k % 8 == 0 and (last - k) % 8 == 0:

            def eight(i):
                for n in range(8):
                    one(8 * i + n, n % 2)

            loop(k // 8, last // 8, eight)
        else:
            for kk in range(k, last):
                one(kk, kk % 2)

    def send_right(qt, halves):
        both = right[qt, 0:16, :] + right[qt, 16:32, :]
        for h, d in halves:
            i = slot_of[d]
            rsend[i] = both[:, h * 128 : h * 128 + 128]
            if d > 0:
                send(3, rsend.at[i], rrx.at[d - 1], in_column(d))
            else:
                send(11, rsend.at[i], hub_rx.at[-d - quarter - 1], in_column(d + quarter))

    def window(kind, src, rx):
        loop(1, quarter + 1, lambda i: send(kind, src, rx.at[i - 1], in_column(i)))
        loop(1, quarter, lambda i: send(kind, src, rx.at[quarter - 1 + i], in_column(-i)))

    def window_sum(kind, own, rx):
        wait(recv_sem, kind, rx)
        total = own
        for i in range(2 * quarter - 1):
            total = total + rx[i]
        return total

    def both_windows(kind, src, rx):
        send(kind, src, rx.at[0], in_column(quarter))
        send(kind, src, rx.at[1], in_column(-quarter))

    def gram_stage(stage):
        if stage == 0:
            wait(recv_sem, 2, g_rx.at[pl.ds(1, npl - 1)])
            total = g_send[s]
            for j in range(1, npl):
                total = total + g_rx[j]
            g_piece[...] = total
            window(4, g_piece, g_zx)
        elif stage == 1:
            g_window[...] = window_sum(4, g_piece[...], g_zx)
            both_windows(13, g_window, g_zy)
        elif stage == 2:
            wait(recv_sem, 13, g_zy)
            total = g_zy[0] + g_zy[1]
            g_tot[...] = total
            g_all[s] = total
            loop(1, npl, lambda j: send(5, g_tot, g_all.at[s], in_plane(j)))
        else:
            wait(recv_sem, 5, g_rx.at[pl.ds(1, npl - 1)])
            eye = lax.broadcasted_iota(jnp.int32, (128, 128), 0) == lax.broadcasted_iota(jnp.int32, (128, 128), 1)
            gram = jnp.concatenate([g_all[i, 0:g_rows, :] for i in range(npl)], axis=0)
            core_ref[...] = gram + jnp.where(eye, noise, 0.0)

    lane128 = lax.broadcasted_iota(jnp.int32, (128, 128), 1)
    sub128 = lax.broadcasted_iota(jnp.int32, (128, 128), 0)

    def sweep(k):
        m = core_ref[...]
        line = core_ref[pl.ds(k, 1), :]
        column = jnp.sum(jnp.where(lane128 == k, m, 0.0), axis=1, keepdims=True)
        pivot = jnp.sum(jnp.where(lane128[0:1] == k, line, 0.0), axis=1, keepdims=True)
        inv = 1.0 / pivot
        line = line * inv
        new = jnp.where(sub128 == k, line, m - column * line)
        core_ref[...] = jnp.where(lane128 == k, jnp.where(sub128 == k, -inv, column * inv), new)

    take_z(pairs[0][0], into(0, 0))
    if pairs[0][1] > 0:
        take_z(pairs[0][1], into(0, 1))
    wait(recv_sem, 15, hub_item)
    for d in sorted((d for d in shifts if d < 0), key=lambda d: (d not in pairs[0], d)):
        give_z(hub_item, d, in_column(-d - quarter))
    if pairs[0][1] < 0:
        take_z(pairs[0][1], into(0, 1))
    steps(0, tp // 2, prepare_even)
    gram_stage(0)
    steps(tp // 2, tp, prepare_odd)
    take_z(half_shift, into(1, 1))
    end = tp + tp // 2
    steps(tp, end)
    send_right(0, ((0, pairs[0][0]), (1, pairs[0][1])))
    middle = lanes(npl // 4 * 128, 128)
    hi, lo = split2(matern(dot(bt[1], a_mat[:, middle])))
    d_p = dp[:, middle]
    right[1] += dot_nt(d_p, hi) + dot_nt(d_p, lo)
    for n, pair in enumerate(pairs[1:]):
        take_z(pair[0], into(2 + n, 0))
        take_z(pair[1], into(2 + n, 1))
        steps(end, end + tp // 2)
        if n == 0:
            send_right(1, ((1, half_shift),))
        else:
            send_right(1 + n, ((0, pairs[n][0]), (1, pairs[n][1])))
        gram_stage(1 + n)
        steps(end + tp // 2, end + tp)
        end += tp
    take_z(single, into_f)
    elementwise((end - 1) % 2)
    apply(end - 2, end % 2)
    apply(end - 1, (end - 1) % 2)
    if len(pairs) > 1:
        send_right(len(pairs), ((0, pairs[-1][0]), (1, pairs[-1][1])))
    else:
        send_right(1, ((1, half_shift),))
        gram_stage(1)
        gram_stage(2)

    fbufs = ((ft_a, fh_a, fl_a), (ft_b, fh_b, fl_b))

    def f_cross(k, par):
        fbufs[par][0][...] = dot(btf[...], a_mat[:, lanes(k * 512 + 128, 512)])

    def f_elementwise(par):
        t, h, l = fbufs[par]
        h[...], l[...] = split2(matern(t[...]))

    def f_apply(k, par, last=False):
        _, h, l = fbufs[par]
        d_q, d_p = dqf[...], dp[:, lanes(k * 512 + 128, 512)]
        hi, lo = h[...], l[...]
        out = dot(d_q, hi) + dot(d_q, lo)
        right_f[...] += dot_nt(d_p, hi) + dot_nt(d_p, lo)
        for i in range(4):
            j = k * 4 + 1 + i
            mine = last and i == 3
            total = out[0:16, i * 128 : i * 128 + 128] + out[16:32, i * 128 : i * 128 + 128]
            at = slice(0, 128) if mine else lanes(j * 128, 128)
            for qt in range(left.shape[0]):
                if not (mine and qt == 1) and not (qt == 0 and not pairs):
                    total = total + (left[qt, 0:16, at] + left[qt, 16:32, at])
            lsend[j] = total
            if not mine:
                slot = 2 * rem(j, half_np) + div(j, half_np)
                send(6, lsend.at[j], lrx.at[npl - slot], in_plane(-slot))

    count = npl // 4

    def f_one(k, par):
        f_apply(k - 2, par)
        f_elementwise(1 - par)
        f_cross(k, par)

    f_cross(0, 0)
    f_elementwise(0)
    if count > 1:
        f_cross(1, 1)

        def f_two(i):
            f_one(2 * i, 0)
            f_one(2 * i + 1, 1)

        loop(1, count // 2, f_two)
        f_elementwise((count - 1) % 2)
        f_apply(count - 2, count % 2)
    f_apply(count - 1, (count - 1) % 2, last=True)
    i = slot_of[single]
    rsend[i] = right_f[0:16, :] + right_f[16:32, :]
    send(3, rsend.at[i], rrx.at[single - 1], in_column(single))
    wait(recv_sem, 11, hub_rx)
    total = hub_rx[0]
    for i in range(1, quarter):
        total = total + hub_rx[i]
    hub_out[...] = total
    send(12, hub_out, hub_in, in_column(-quarter))
    gram_stage(3)
    loop(0, 16, sweep)

    wait(recv_sem, 6, lrx.at[pl.ds(1, npl - 1)])
    wait(recv_sem, 3, rrx)
    total = lsend[npl] + (right[1, 0:16, 0:128] + right[1, 16:32, 0:128])
    for j in range(1, npl):
        total = total + lrx[j]
    for i in range(quarter):
        total = total + rrx[i]
    wait(recv_sem, 12, hub_in)
    total = total + hub_in[...]
    image = (var_ref[0] * POLY) * total + noise * direction

    proj_im = lax.dot_general(image, factor, NT, precision=highest, preferred_element_type=F32)
    products = ((direction, image), (residual, image), (image, image), (residual, residual))
    scalars = jnp.zeros((16, 128), F32)
    for n, (a, b) in enumerate(products):
        scalars = jnp.where(lane16 == rem(sub16, 8) * 4 + n, jnp.sum(a * b, axis=1, keepdims=True), scalars)

    for c in range(2):
        for p in range(8):
            v_half[c, p] = proj_im[8 * c + p : 8 * c + p + 1]
        v_half[c, 8] = jnp.sum(scalars[8 * c : 8 * c + 8], axis=0, keepdims=True)
    loop(1, npl, lambda j: send(8, v_half.at[rem(s + j, 2)], v_px.at[j], in_plane(j)))
    loop(16, 60, sweep)
    wait(recv_sem, 8, v_px.at[pl.ds(1, npl - 1)])
    total = v_half[core]
    for j in range(1, npl):
        total = total + v_px[j]
    v_plane[...] = total
    window(9, v_plane, v_zx)
    loop(60, 96, sweep)
    v_window[...] = window_sum(9, v_plane[...], v_zx)
    for other in (0, 1):
        send(14, v_window, v_zy.at[core, 0], in_column(quarter, other))
        send(14, v_window, v_zy.at[core, 1], in_column(-quarter, other))
    loop(96, 128, sweep)
    core_inv = -core_ref[...]
    both_inv = jnp.concatenate(
        [core_inv, jnp.dot(core_inv, factor, precision=highest, preferred_element_type=F32)], axis=1
    )
    proj_re = jnp.zeros((16, 128), F32)
    for p in range(probes):
        at = g_rows + p % per
        proj_re = jnp.where(sub16 == p, g_all[p // per, at : at + 1, :], proj_re)
    of_re = jnp.dot(proj_re, both_inv, precision=highest, preferred_element_type=F32)
    wait(recv_sem, 14, v_zy)
    for h in range(2):
        v_all[h] = v_zy[h, 0] + v_zy[h, 1]
    proj_im = jnp.zeros((16, 128), F32)
    for p in range(probes):
        proj_im = jnp.where(sub16 == p, v_all[p // 8, p % 8], proj_im)
    inner = jnp.where(sub16 < 8, v_all[0, 8], v_all[1, 8])
    d_im, r_im, im_im, r_r = (
        jnp.sum(jnp.where(lane16 == rem(sub16, 8) * 4 + n, inner, 0.0), axis=1, keepdims=True) for n in range(4)
    )
    of_im = jnp.dot(proj_im, both_inv, precision=highest, preferred_element_type=F32)
    coef_re, coef_im = of_re[:, 0:128], of_im[:, 0:128]
    res_z = (r_r - jnp.sum(proj_re * coef_re, axis=1, keepdims=True)) / noise
    alpha = res_z / d_im
    coef_new = coef_re - alpha * coef_im
    proj_new = proj_re - alpha * proj_im
    new_sq = r_r - 2.0 * alpha * r_im + alpha * alpha * im_im
    res_z_new = (new_sq - jnp.sum(proj_new * coef_new, axis=1, keepdims=True)) / noise
    beta = res_z_new / res_z
    new_residual = residual - alpha * image
    sol_out[...] = solution_ref[...] + alpha * direction
    res_out[...] = new_residual
    fitted = of_re[:, 128:256] - alpha * of_im[:, 128:256]
    dir_out[...] = (new_residual - fitted) / noise + beta * direction

    wait(send_sem, 0, items.at[pl.ds(1, npl - 1)])
    wait(send_sem, 1, zitems)
    wait(send_sem, 2, g_rx.at[pl.ds(1, npl - 1)])
    wait(send_sem, 3, rrx)
    wait(send_sem, 4, g_zx)
    wait(send_sem, 5, g_rx.at[pl.ds(1, npl - 1)])
    wait(send_sem, 6, lrx.at[pl.ds(1, npl - 1)])
    wait(send_sem, 8, v_px.at[pl.ds(1, npl - 1)])
    wait(send_sem, 9, v_zx)
    wait(send_sem, 11, hub_rx)
    wait(send_sem, 12, hub_in)
    wait(send_sem, 13, g_zy)
    wait(send_sem, 14, v_zy)
    wait(send_sem, 15, hub_item)


def hand_out(*refs):
    for src, dst in zip(refs[:3], refs[3:]):
        dst[...] = src[...]


def local(points, lengthscales, variances, factor, solution, residual, direction):
    nz, npl = Z_HI * Z_LO, X * Y * 2
    quarter = nz // 4
    blocks, nq = 2 * quarter, quarter
    gr, vr = -(-(128 // npl + max(16 // npl, 1)) // 8) * 8, (9, 1, 128)
    wide = (npl + 1) * 128
    vmem = pl.BlockSpec(memory_space=pltpu.VMEM)
    held = [pltpu.VMEM, pltpu.SMEM, pltpu.SMEM, pltpu.VMEM, pltpu.VMEM, pltpu.VMEM, pltpu.VMEM]
    args = (points, lengthscales, variances, factor, solution, residual, direction)
    tile, ftile = (256, 256), (128, 512)
    scratch = [
        ((32, 128), F32), ((npl, 32, 128), F32), ((blocks, 32, 128), F32), ((32, 128), F32),
        ((128, wide), BF16), ((32, wide), BF16), ((nq, 256, 128), BF16), ((nq, 32, 256), BF16),
        ((128, 128), BF16), ((32, 128), BF16),
        (tile, F32), (tile, F32), (tile, BF16), (tile, BF16), (tile, BF16), (tile, BF16),
        (ftile, F32), (ftile, F32), (ftile, BF16), (ftile, BF16), (ftile, BF16), (ftile, BF16),
        ((nq, 32, npl * 128), F32), ((nq, 32, 256), F32), ((32, 128), F32),
        ((npl + 1, 16, 128), F32), ((npl, 16, 128), F32), ((blocks, 16, 128), F32), ((quarter, 16, 128), F32),
        ((quarter, 16, 128), F32), ((16, 128), F32), ((16, 128), F32),
        ((npl, gr, 128), F32), ((npl, gr, 128), F32), ((gr, 128), F32), ((blocks - 1, gr, 128), F32),
        ((gr, 128), F32), ((2, gr, 128), F32),
        ((gr, 128), F32), ((npl, gr, 128), F32), ((128, 128), F32),
        ((2, *vr), F32), ((npl, *vr), F32), (vr, F32), ((blocks - 1, *vr), F32), (vr, F32),
        ((2, 2, *vr), F32), ((2, *vr), F32),
    ]
    out = jax.ShapeDtypeStruct(direction.shape, F32)
    outs = pl.pallas_call(
        kernel,
        out_shape=(out, out, out),
        in_specs=[pl.BlockSpec(memory_space=pl.ANY)] * len(args),
        out_specs=(vmem, vmem, vmem),
        scratch_shapes=[space(a.shape, F32) for space, a in zip(held, args)]
        + [pltpu.VMEM(shape, dtype) for shape, dtype in scratch]
        + [pltpu.SemaphoreType.DMA((n,)) for n in (len(args), 16, 16 + blocks, npl)],
        compiler_params=pltpu.CompilerParams(
            collective_id=0, has_side_effects=True, vmem_limit_bytes=56 * 2**20
        ),
    )(*args)
    return pl.pallas_call(
        hand_out,
        out_shape=(out, out, out),
        in_specs=[vmem] * 3,
        out_specs=(vmem, vmem, vmem),
    )(*outs)


def solution(mesh):
    placed = P(None, ("row", "col"))
    return jax.shard_map(
        local,
        mesh=mesh,
        in_specs=(placed, P(), P(), placed, placed, placed, placed),
        out_specs=(placed, placed, placed),
        check_vma=False,
    )
```
